256 devices in a mesh: row: 32 (over x, z_lo, core), col: 8 (over y, z_hi).
Axes of the slice: x: 4, y: 4, z: 8 (z_hi: 2, z_lo: 4; z = z_hi * 4 + z_lo), core: 2. Of those that a mesh axis runs over, the one named last changes fastest.
Arguments:
- tokens: bfloat16 [512, 8192], P('col', 'row'), may hold values from -6 to 6
- gate_weight: bfloat16 [8192, 28672], P('row', 'col'), may hold values from -0.0625 to 0.0625
- up_weight: bfloat16 [8192, 28672], P('row', 'col'), may hold values from -0.0625 to 0.0625
- down_weight: bfloat16 [28672, 8192], P('col', 'row'), may hold values from -0.03125 to 0.03125
- out_grad: bfloat16 [512, 8192], P('col', 'row'), may hold values from -6 to 6
Outputs:
- layer_out: bfloat16 [512, 8192], P('col', 'row')
- token_grad: bfloat16 [512, 8192], P('col', 'row')
- gate_grad: bfloat16 [8192, 28672], P('row', 'col')
- up_grad: bfloat16 [8192, 28672], P('row', 'col')
- down_grad: bfloat16 [28672, 8192], P('col', 'row')
The draws below stay inside these ranges and needn't reach their ends.
All inputs are finite; a program needn't handle non-finite values.
Results may differ from the reference program's by a relative error of at most 0.0067.
Values may be sent and summed in bfloat16 or wider, within the bound.
A program may use at most 128 MiB of HBM per device.

```python
import jax
import jax.numpy as jnp

D = 8192
FF = 28672
TOKENS = 512


def spiked(entries, stream_key, source, target, parts, factor):
    owner, partner = [(jnp.arange(entries.shape[position]) // (entries.shape[position] // parts)).reshape([-1 if axis == position else 1 for axis in range(entries.ndim)]) for position in (source, target)]
    chosen = jax.random.permutation(stream_key, parts)[partner]
    strong = (owner == chosen) | (owner == (partner + parts // 2) % parts)
    return jnp.where(strong, factor * entries, entries)


def block_levels(key, shape, pieces, smallest, largest):
    factor_of = 1.0
    for axis_at, shards_of in pieces:
        draws = jax.random.uniform(jax.random.fold_in(jax.random.fold_in(key, 6), axis_at), (shards_of,), jnp.float32, smallest / len(pieces), largest / len(pieces))
        factor_of = factor_of * jnp.repeat(jnp.exp(draws), shape[axis_at] // shards_of).reshape((-1,) + (1,) * (len(shape) - 1 - axis_at))
    return factor_of


def noise(key, extent, spread, most, shards=(), dtype=jnp.bfloat16):
    array = spread * jax.random.normal(key, extent, jnp.float32)
    if shards:
        array = array * block_levels(key, extent, shards, -0.22, 0.18)
    return jnp.clip(array, -most, most).astype(dtype)


def gaussian_with(rng, shape, width, reach, pieces, heavy, held_as=jnp.bfloat16):
    array = width * jax.random.normal(rng, shape, jnp.float32)
    if pieces:
        array = array * block_levels(rng, shape, pieces, -0.22, 0.18)
    return jnp.clip(spiked(array, jax.random.fold_in(rng, 3), *heavy), -reach, reach).astype(held_as)


def setup_inputs(seed: int = 0) -> dict:
    seeds = jax.random.split(jax.random.key(seed), 6)
    return {
        "tokens": gaussian_with(seeds[0], (TOKENS, D), 1.0, 6.0, ((0, 8), (1, 32)), (1, 0, 32, 2.75)),
        "gate_weight": noise(seeds[1], (D, FF), D ** -0.5, 0.0625, ((0, 32), (1, 8))),
        "up_weight": noise(seeds[2], (D, FF), D ** -0.5, 0.0625, ((0, 32), (1, 8))),
        "down_weight": noise(seeds[3], (FF, D), FF ** -0.5, 0.03125, ((0, 8), (1, 32))),
        "out_grad": gaussian_with(seeds[4], (TOKENS, D), 1.0, 6.0, ((0, 8), (1, 32)), (1, 0, 32, 2.75)),
    }


def reference(tokens, gate_weight, up_weight, down_weight, out_grad):
    gate = jnp.dot(tokens, gate_weight, preferred_element_type=jnp.float32).astype(jnp.bfloat16)
    up = jnp.dot(tokens, up_weight, preferred_element_type=jnp.float32).astype(jnp.bfloat16)
    gate_value = gate.astype(jnp.float32)
    up_value = up.astype(jnp.float32)
    sigma = jax.nn.sigmoid(gate_value)
    hidden = (gate_value * sigma * up_value).astype(jnp.bfloat16)
    layer_out = jnp.dot(hidden, down_weight, preferred_element_type=jnp.float32).astype(jnp.bfloat16)
    down_grad = jnp.dot(hidden.T, out_grad, preferred_element_type=jnp.float32).astype(jnp.bfloat16)
    hidden_grad = jnp.dot(out_grad, down_weight.T, preferred_element_type=jnp.float32)
    gate_delta = (hidden_grad * up_value * sigma * (1.0 + gate_value * (1.0 - sigma))).astype(jnp.bfloat16)
    up_delta = (hidden_grad * gate_value * sigma).astype(jnp.bfloat16)
    token_grad = (jnp.dot(gate_delta, gate_weight.T, preferred_element_type=jnp.float32)
                  + jnp.dot(up_delta, up_weight.T, preferred_element_type=jnp.float32)).astype(jnp.bfloat16)
    gate_grad = jnp.dot(tokens.T, gate_delta, preferred_element_type=jnp.float32).astype(jnp.bfloat16)
    up_grad = jnp.dot(tokens.T, up_delta, preferred_element_type=jnp.float32).astype(jnp.bfloat16)
    return (layer_out, token_grad, gate_grad, up_grad, down_grad)
```

```python
import jax
import jax.numpy as jnp
from jax import lax
from jax.experimental import pallas as pl
from jax.experimental.pallas import tpu as pltpu
from jax.sharding import PartitionSpec as P

MESH = pl.DeviceIdType.MESH
BF = jnp.bfloat16
F32 = jnp.float32
NP = 7
W = 256
HALF = NP * W
F = 256


def dot(a, b, dims):
    return lax.dot_general(a, b, (dims, ((), ())), preferred_element_type=F32)


NN = ((1,), (0,))
NT = ((1,), (1,))
TN = ((0,), (0,))


def kernel(
    tok, gate_w, up_w, down_w, cot,
    lo_ref, tg_ref, gate_g, up_g, down_g,
    tc, wgu, wd, s32, sb, r1, a2, r2, yb, zr, ag, go, do, acc, e1b, e2b, e2r, e3b, e3r,
    in_l, wl, ws, wr, zh_s, zh_r, y_s, y_r, co_s, co_r,
    x_s, x_r, z_s, z_r, za_s, za_r, xa_s, xa_r, ol, os_, or_,
    e1_s, e1_r, e2_s, e2_r, e3_s, e3_r,
):
    row, col = lax.axis_index("row"), lax.axis_index("col")
    x, zl, c = row // 8, (row // 2) % 4, row % 2
    y, zh = col // 2, col % 2
    xp, xm, x2 = (x + 1) % 4, (x + 3) % 4, (x + 2) % 4

    def at_x(px):
        return (px * 8 + zl * 2 + c, col)

    def z_of(dz):
        b = (zl % 2) if dz % 2 == 0 else 1 - zl % 2
        h = (zl // 2) if dz < 2 else 1 - zl // 2
        return h * 2 + b

    def at_z(dz):
        return (x * 8 + z_of(dz) * 2 + c, col)

    def at_y(dy):
        return (row, ((y + dy) % 4) * 2 + zh)

    at_co = (x * 8 + zl * 2 + 1 - c, col)
    at_zh = (row, y * 2 + 1 - zh)
    peers = [at_co, at_zh, at_x(xp), at_x(xm)]
    peers += [at_z(d) for d in (1, 2, 3)] + [at_y(d) for d in (1, 2, 3)]

    def remote(src, dst, ss, rs, dev):
        return pltpu.make_async_remote_copy(
            src_ref=src, dst_ref=dst, send_sem=ss, recv_sem=rs, device_id=dev, device_id_type=MESH
        )

    def cols(core, k):
        return pl.ds(pl.multiple_of(core * HALF + k * W, W), W)

    def feats(core):
        return pl.ds(pl.multiple_of(core * F, F), F)

    def rows(start, size):
        return pl.ds(pl.multiple_of(start, size), size)

    def w_local(k):
        return (
            pltpu.make_async_copy(gate_w.at[:, cols(c, k)], wgu.at[k, feats(c), pl.ds(0, W)], wl.at[k, 0]),
            pltpu.make_async_copy(up_w.at[:, cols(c, k)], wgu.at[k, feats(c), pl.ds(W, W)], wl.at[k, 1]),
            pltpu.make_async_copy(down_w.at[cols(c, k), :], wd.at[k, :, feats(c)], wl.at[k, 2]),
        )

    def w_remote(k):
        o = 1 - c
        return (
            remote(gate_w.at[:, cols(o, k)], wgu.at[k, feats(c), pl.ds(0, W)], ws.at[k, 0], wr.at[k, 0], at_co),
            remote(up_w.at[:, cols(o, k)], wgu.at[k, feats(c), pl.ds(W, W)], ws.at[k, 1], wr.at[k, 1], at_co),
            remote(down_w.at[cols(o, k), :], wd.at[k, :, feats(c)], ws.at[k, 2], wr.at[k, 2], at_co),
        )

    def block(j):
        return tc.at[:, rows(j * 64, 64), feats(c)]

    def b_zh():
        return remote(block(col), block(col), zh_s, zh_r, at_zh)

    def b_y(h, dy):
        b = block(y * 2 + (zh if h == 0 else 1 - zh))
        return remote(b, b, y_s.at[h, dy - 1], y_r.at[h, dy - 1], at_y(dy))

    def b_co(j):
        return remote(block(j), block(j), co_s.at[j], co_r.at[j], at_co)

    ins = (
        pltpu.make_async_copy(tok, tc.at[0, rows(col * 64, 64), feats(c)], in_l.at[0]),
        pltpu.make_async_copy(cot, tc.at[1, rows(col * 64, 64), feats(c)], in_l.at[1]),
    )
    for d in ins:
        d.start()

    @pl.loop(0, NP)
    def _(k):
        for d in w_local(k):
            d.start()

    barrier = pltpu.get_barrier_semaphore()
    for p in peers:
        pl.semaphore_signal(barrier, inc=1, device_id=p, device_id_type=MESH)
    pl.semaphore_wait(barrier, len(peers))

    for d in ins:
        d.wait()
    b_zh().start()
    for dy in (1, 2, 3):
        b_y(0, dy).start()
    b_co(col).start()

    @pl.loop(0, NP)
    def _(k):
        for d in w_remote(k):
            d.start()

    acc[...] = jnp.zeros_like(acc)
    b_zh().wait_recv()
    for dy in (1, 2, 3):
        b_y(1, dy).start()
    b_co(y * 2 + 1 - zh).start()
    for h in (0, 1):
        for dy in (1, 2, 3):
            b_y(h, dy).wait_recv()
            b_co(((y + 4 - dy) % 4) * 2 + (zh if h == 0 else 1 - zh)).start()

    @pl.loop(0, 8)
    def _(j):
        b_co(j).wait_recv()

    def chunk(px):
        return pl.multiple_of(px * 128, 128)

    def x_copy(k, i):
        if i == 0:
            src, dst, to = sb.at[k, rows(chunk(x2), 64)], r1.at[k, 0], xp
        elif i == 1:
            src, dst, to = sb.at[k, rows(chunk(x2) + 64, 64)], r1.at[k, 1], xm
        elif i == 2:
            src, dst, to = sb.at[k, rows(chunk(xp) + 64, 64)], r2.at[k, 0, pl.ds(64, 64)], xp
        elif i == 3:
            src, dst, to = sb.at[k, rows(chunk(xm), 64)], r2.at[k, 1, pl.ds(0, 64)], xm
        elif i == 4:
            src, dst, to = a2.at[k, 0], r2.at[k, 0, pl.ds(0, 64)], xp
        else:
            src, dst, to = a2.at[k, 1], r2.at[k, 1, pl.ds(64, 64)], xm
        return remote(src, dst, x_s.at[k, i], x_r.at[k, i], at_x(to))

    def z_copy(k, dz):
        src = yb.at[k, rows(z_of(dz) * 32, 32)]
        return remote(src, zr.at[k, dz - 1], z_s.at[k, dz - 1], z_r.at[k, dz - 1], at_z(dz))

    def za_copy(k, dz):
        mine = ag.at[k, rows(x * 128 + zl * 32, 32)]
        return remote(mine, mine, za_s.at[k, dz - 1], za_r.at[k, dz - 1], at_z(dz))

    def xa_copy(k, i):
        if i < 2:
            part, to = ag.at[k, rows(chunk(x), 128)], (xp, xm)[i]
        elif i == 2:
            part, to = ag.at[k, rows(chunk(xm), 64)], xp
        else:
            part, to = ag.at[k, rows(chunk(xp) + 64, 64)], xm
        return remote(part, part, xa_s.at[k, i], xa_r.at[k, i], at_x(to))

    def out_local(k):
        return (
            pltpu.make_async_copy(go.at[k, feats(c), pl.ds(0, W)], gate_g.at[:, cols(c, k)], ol.at[k, 0]),
            pltpu.make_async_copy(go.at[k, feats(c), pl.ds(W, W)], up_g.at[:, cols(c, k)], ol.at[k, 1]),
            pltpu.make_async_copy(do.at[k, :, feats(c)], down_g.at[cols(c, k), :], ol.at[k, 2]),
        )

    def out_remote(k):
        o = 1 - c
        return (
            remote(go.at[k, feats(o), pl.ds(0, W)], gate_g.at[:, cols(c, k)], os_.at[k, 0], or_.at[k, 0], at_co),
            remote(go.at[k, feats(o), pl.ds(W, W)], up_g.at[:, cols(c, k)], os_.at[k, 1], or_.at[k, 1], at_co),
            remote(do.at[k, :, feats(o)], down_g.at[cols(c, k), :], os_.at[k, 2], or_.at[k, 2], at_co),
        )

    def s0(k):
        for d in w_local(k):
            d.wait()
        for d in w_remote(k):
            d.wait_recv()
        b = k % 4
        p = dot(tc[0], wgu[k], NN)
        s32[b, :, : 2 * W] = p
        sb[k, :, : 2 * W] = p.astype(BF)
        q = dot(tc[1], wd[k], NT)
        s32[b, :, 2 * W :] = q
        sb[k, :, 2 * W :] = q.astype(BF)
        for i in range(4):
            x_copy(k, i).start()

    def s1(k):
        b = k % 4
        x_copy(k, 0).wait_recv()
        a2[k, 0] = (s32[b, rows(chunk(xp), 64)] + r1[k, 0].astype(F32)).astype(BF)
        x_copy(k, 4).start()
        x_copy(k, 1).wait_recv()
        a2[k, 1] = (s32[b, rows(chunk(xm) + 64, 64)] + r1[k, 1].astype(F32)).astype(BF)
        x_copy(k, 5).start()

    def s2(k):
        b = k % 4
        for i in (2, 3, 4, 5):
            x_copy(k, i).wait_recv()
        total = s32[b, rows(chunk(x), 128)] + (r2[k, 0].astype(F32) + r2[k, 1].astype(F32))
        s32[b, rows(chunk(x), 128)] = total
        yb[k] = total.astype(BF)
        for dz in (2, 1, 3):
            z_copy(k, dz).start()

    def s3(k):
        b = k % 4
        for dz in (1, 2, 3):
            z_copy(k, dz).wait_recv()
        total = s32[b, rows(chunk(x) + zl * 32, 32)]
        for i in range(3):
            total = total + zr[k, i].astype(F32)
        g = total[:, :W]
        u = total[:, W : 2 * W]
        hg = total[:, 2 * W :]
        s = 1.0 / (1.0 + jnp.exp(-g))
        here = rows(x * 128 + zl * 32, 32)
        ag[k, here, :W] = (hg * u * s * (1.0 + g * (1.0 - s))).astype(BF)
        ag[k, here, W : 2 * W] = (hg * g * s).astype(BF)
        ag[k, here, 2 * W :] = (g * s * u).astype(BF)
        for dz in (2, 1, 3):
            za_copy(k, dz).start()

    def s4(k):
        for dz in (1, 2, 3):
            za_copy(k, dz).wait_recv()
        xa_copy(k, 0).start()
        xa_copy(k, 1).start()

    def s5(k):
        xa_copy(k, 0).wait_recv()
        xa_copy(k, 2).start()
        xa_copy(k, 1).wait_recv()
        xa_copy(k, 3).start()

    def s6(k):
        xa_copy(k, 2).wait_recv()
        xa_copy(k, 3).wait_recv()
        go[k] = dot(tc[0], ag[k, :, : 2 * W], TN).astype(BF)
        do[k] = dot(ag[k, :, 2 * W :], tc[1], TN).astype(BF)
        for d in out_remote(k):
            d.start()
        for d in out_local(k):
            d.start()
        acc[1] += dot(ag[k, :, : 2 * W], wgu[k], NT)
        acc[0] += dot(ag[k, :, 2 * W :], wd[k], NN)

    @pl.loop(0, NP + 6)
    def _(t):
        for lag, stage in ((0, s0), (1, s1), (2, s2), (3, s3), (4, s4), (5, s5), (6, s6)):
            k = t - lag

            @pl.when((k >= 0) & (k < NP))
            def _(k=k, stage=stage):
                stage(k)

    def e1(i):
        return remote(acc.at[i, :, feats(1 - c)], e1b.at[i], e1_s.at[i], e1_r.at[i], at_co)

    def e2(dy):
        src = e2b.at[:, rows(((y + dy) % 4) * 128, 128)]
        return remote(src, e2r.at[dy - 1], e2_s.at[dy - 1], e2_r.at[dy - 1], at_y(dy))

    def e3():
        return remote(e3b, e3r, e3_s, e3_r, at_zh)

    for i in (0, 1):
        e1(i).start()
    for i in (0, 1):
        e1(i).wait_recv()
        total = acc[i, :, feats(c)] + e1b[i]
        e1b[i] = total
        e2b[i] = total.astype(BF)
    for dy in (2, 1, 3):
        e2(dy).start()
    for dy in (1, 2, 3):
        e2(dy).wait_recv()
    there, mine = rows(y * 128 + (1 - zh) * 64, 64), rows(y * 128 + zh * 64, 64)
    rt, rm = rows((1 - zh) * 64, 64), rows(zh * 64, 64)
    away = e1b[:, there]
    for i in range(3):
        away = away + e2r[i, :, rt].astype(F32)
    e3b[...] = away.astype(BF)
    e3().start()
    kept = e1b[:, mine]
    for i in range(3):
        kept = kept + e2r[i, :, rm].astype(F32)
    e3().wait_recv()
    kept = (kept + e3r[...].astype(F32)).astype(BF)
    lo_ref[...] = kept[0]
    tg_ref[...] = kept[1]

    b_zh().wait_send()
    for h in (0, 1):
        for dy in (1, 2, 3):
            b_y(h, dy).wait_send()

    @pl.loop(0, 8)
    def _(j):
        b_co(j).wait_send()

    @pl.loop(0, NP)
    def _(k):
        for d in w_remote(k):
            d.wait_send()
        for i in range(6):
            x_copy(k, i).wait_send()
        for dz in (1, 2, 3):
            z_copy(k, dz).wait_send()
            za_copy(k, dz).wait_send()
        for i in range(4):
            xa_copy(k, i).wait_send()
        for d in out_local(k):
            d.wait()
        for d in out_remote(k):
            d.wait()

    for i in (0, 1):
        e1(i).wait_send()
    for dy in (1, 2, 3):
        e2(dy).wait_send()
    e3().wait_send()


def local(tokens, gate_weight, up_weight, down_weight, out_grad):
    def v(*shape, t=BF):
        return pltpu.VMEM(shape, t)

    def sem(*shape):
        return pltpu.SemaphoreType.DMA(shape) if shape else pltpu.SemaphoreType.DMA

    W3 = 3 * W
    anywhere = pl.BlockSpec(memory_space=pl.ANY)
    vmem = pl.BlockSpec(memory_space=pltpu.VMEM)
    macs = 9 * 512 * 256 * 3584
    return pl.pallas_call(
        kernel,
        out_shape=(
            jax.ShapeDtypeStruct((64, 256), BF),
            jax.ShapeDtypeStruct((64, 256), BF),
            jax.ShapeDtypeStruct((256, 3584), BF),
            jax.ShapeDtypeStruct((256, 3584), BF),
            jax.ShapeDtypeStruct((3584, 256), BF),
        ),
        in_specs=[anywhere] * 5,
        out_specs=(vmem, vmem, anywhere, anywhere, anywhere),
        scratch_shapes=[
            v(2, 512, 512),
            v(NP, 512, 2 * W),
            v(NP, W, 512),
            v(4, 512, W3, t=F32),
            v(NP, 512, W3),
            v(NP, 2, 64, W3),
            v(NP, 2, 64, W3),
            v(NP, 2, 128, W3),
            v(NP, 128, W3),
            v(NP, 3, 32, W3),
            v(NP, 512, W3),
            v(NP, 512, 2 * W),
            v(NP, W, 512),
            v(2, 512, 512, t=F32),
            v(2, 512, 256, t=F32),
            v(2, 512, 256),
            v(3, 2, 128, 256),
            v(2, 64, 256),
            v(2, 64, 256),
            sem(2), sem(NP, 3), sem(NP, 3), sem(NP, 3),
            sem(), sem(), sem(2, 3), sem(2, 3), sem(8), sem(8),
            sem(NP, 6), sem(NP, 6), sem(NP, 3), sem(NP, 3),
            sem(NP, 3), sem(NP, 3), sem(NP, 4), sem(NP, 4),
            sem(NP, 3), sem(NP, 3), sem(NP, 3),
            sem(2), sem(2), sem(3), sem(3), sem(), sem(),
        ],
        compiler_params=pltpu.CompilerParams(
            collective_id=0, has_side_effects=True, vmem_limit_bytes=60 * 2**20
        ),
        cost_estimate=pl.CostEstimate(flops=2 * macs, bytes_accessed=12 * 2**20, transcendentals=2**16),
        name="swiglu",
    )(tokens, gate_weight, up_weight, down_weight, out_grad)


def solution(mesh):
    tokens, weights = P("col", "row"), P("row", "col")
    return jax.shard_map(
        local,
        mesh=mesh,
        in_specs=(tokens, weights, weights, tokens, tokens),
        out_specs=(tokens, tokens, weights, weights, tokens),
        check_vma=False,
    )
```

```python
import jax
import jax.numpy as jnp
from jax import lax
from jax.experimental import pallas as pl
from jax.experimental.pallas import tpu as pltpu
from jax.sharding import PartitionSpec as P

MESH = pl.DeviceIdType.MESH
BF = jnp.bfloat16
F32 = jnp.float32
NP = 7
W = 256
AHEAD = 2
HALF = NP * W
F = 256


def dot(a, b, dims):
    return lax.dot_general(a, b, (dims, ((), ())), preferred_element_type=F32)


NN = ((1,), (0,))
NT = ((1,), (1,))
TN = ((0,), (0,))


def kernel(
    tok, gate_w, up_w, down_w, cot,
    lo_ref, tg_ref, gate_g, up_g, down_g,
    tc, wgu, wd, s32, sb, r1, a2, r2, yb, zr,
    h32, hs, hz1, hb, hr1, ha, hr2, hy, hz2, ag, hg, go, do, acc, e1b, e2b, e2r, e3b, e3r,
    in_l, wl, ws, wr, zh_s, zh_r, y_s, y_r, co_s, co_r,
    x_s, x_r, z_s, z_r, za_s, za_r, xa_s, xa_r, h_s, h_r, ha_s, ha_r, ol, os_, or_,
    e1_s, e1_r, e2_s, e2_r, e3_s, e3_r,
):
    row, col = lax.axis_index("row"), lax.axis_index("col")
    x, zl, c = row // 8, (row // 2) % 4, row % 2
    y, zh = col // 2, col % 2
    xp, xm, x2 = (x + 1) % 4, (x + 3) % 4, (x + 2) % 4

    def at_x(px):
        return (px * 8 + zl * 2 + c, col)

    def z_of(dz):
        b = (zl % 2) if dz % 2 == 0 else 1 - zl % 2
        h = (zl // 2) if dz < 2 else 1 - zl // 2
        return h * 2 + b

    def at_z(dz):
        return (x * 8 + z_of(dz) * 2 + c, col)

    def at_y(dy):
        return (row, ((y + dy) % 4) * 2 + zh)

    at_co = (x * 8 + zl * 2 + 1 - c, col)
    at_zh = (row, y * 2 + 1 - zh)
    peers = [at_co, at_zh, at_x(xp), at_x(xm)]
    peers += [at_z(d) for d in (1, 2, 3)] + [at_y(d) for d in (1, 2, 3)]

    def remote(src, dst, ss, rs, dev):
        return pltpu.make_async_remote_copy(
            src_ref=src, dst_ref=dst, send_sem=ss, recv_sem=rs, device_id=dev, device_id_type=MESH
        )

    def cols(core, k):
        return pl.ds(pl.multiple_of(core * HALF + k * W, W), W)

    def feats(core):
        return pl.ds(pl.multiple_of(core * F, F), F)

    def rows(start, size):
        return pl.ds(pl.multiple_of(start, size), size)

    def w_local(k):
        return (
            pltpu.make_async_copy(gate_w.at[:, cols(c, k)], wgu.at[k, feats(c), pl.ds(0, W)], wl.at[k, 0]),
            pltpu.make_async_copy(up_w.at[:, cols(c, k)], wgu.at[k, feats(c), pl.ds(W, W)], wl.at[k, 1]),
            pltpu.make_async_copy(down_w.at[cols(c, k), :], wd.at[k, :, feats(c)], wl.at[k, 2]),
        )

    def w_remote(k):
        o = 1 - c
        return (
            remote(gate_w.at[:, cols(o, k)], wgu.at[k, feats(c), pl.ds(0, W)], ws.at[k, 0], wr.at[k, 0], at_co),
            remote(up_w.at[:, cols(o, k)], wgu.at[k, feats(c), pl.ds(W, W)], ws.at[k, 1], wr.at[k, 1], at_co),
            remote(down_w.at[cols(o, k), :], wd.at[k, :, feats(c)], ws.at[k, 2], wr.at[k, 2], at_co),
        )

    def block(j):
        return tc.at[:, rows(j * 64, 64), feats(c)]

    def b_zh():
        return remote(block(col), block(col), zh_s, zh_r, at_zh)

    def b_y(h, dy):
        b = block(y * 2 + (zh if h == 0 else 1 - zh))
        return remote(b, b, y_s.at[h, dy - 1], y_r.at[h, dy - 1], at_y(dy))

    def b_co(j):
        return remote(block(j), block(j), co_s.at[j], co_r.at[j], at_co)

    ins = (
        pltpu.make_async_copy(tok, tc.at[0, rows(col * 64, 64), feats(c)], in_l.at[0]),
        pltpu.make_async_copy(cot, tc.at[1, rows(col * 64, 64), feats(c)], in_l.at[1]),
    )
    for d in ins:
        d.start()
    barrier = pltpu.get_barrier_semaphore()
    for p in peers:
        pl.semaphore_signal(barrier, inc=1, device_id=p, device_id_type=MESH)

    @pl.loop(0, NP)
    def _(k):
        for d in w_local(k):
            d.start()

    pl.semaphore_wait(barrier, len(peers))

    for d in ins:
        d.wait()
    b_zh().start()
    for dy in (1, 2, 3):
        b_y(0, dy).start()
    b_co(col).start()
    for k in range(AHEAD):
        for d in w_remote(k):
            d.start()

    acc[...] = jnp.zeros_like(acc)
    b_zh().wait_recv()
    for dy in (1, 2, 3):
        b_y(1, dy).start()
    b_co(y * 2 + 1 - zh).start()
    for h in (0, 1):
        for dy in (1, 2, 3):
            b_y(h, dy).wait_recv()
            b_co(((y + 4 - dy) % 4) * 2 + (zh if h == 0 else 1 - zh)).start()

    @pl.loop(0, 8)
    def _(j):
        b_co(j).wait_recv()

    b0, b1 = zl % 2, zl // 2

    def chunk(px):
        return pl.multiple_of(px * 128, 128)

    def x_copy(k, i):
        if i == 0:
            src, dst, to = sb.at[k, rows(chunk(x2), 64)], r1.at[k, 0], xp
        elif i == 1:
            src, dst, to = sb.at[k, rows(chunk(x2) + 64, 64)], r1.at[k, 1], xm
        elif i == 2:
            src, dst, to = sb.at[k, rows(chunk(xp) + 64, 64)], r2.at[k, 0, pl.ds(64, 64)], xp
        elif i == 3:
            src, dst, to = sb.at[k, rows(chunk(xm), 64)], r2.at[k, 1, pl.ds(0, 64)], xm
        elif i == 4:
            src, dst, to = a2.at[k, 0], r2.at[k, 0, pl.ds(0, 64)], xp
        else:
            src, dst, to = a2.at[k, 1], r2.at[k, 1, pl.ds(64, 64)], xm
        return remote(src, dst, x_s.at[k, i], x_r.at[k, i], at_x(to))

    def z_copy(k, dz):
        src = yb.at[k, rows(z_of(dz) * 32, 32)]
        return remote(src, zr.at[k, dz - 1], z_s.at[k, dz - 1], z_r.at[k, dz - 1], at_z(dz))

    def h_copy(k, i):
        to = xp if i in (1, 3, 5) else xm
        if i == 0:
            src, dst = hs.at[k, :, :, 1 - b0], hz1.at[k]
        elif i == 1:
            src, dst = hb.at[k, x2, 0], hr1.at[k, 0]
        elif i == 2:
            src, dst = hb.at[k, x2, 1], hr1.at[k, 1]
        elif i == 3:
            src, dst = hb.at[k, xp, 1], hr2.at[k, 0, 1]
        elif i == 4:
            src, dst = hb.at[k, xm, 0], hr2.at[k, 1, 0]
        elif i == 5:
            src, dst = ha.at[k, 0], hr2.at[k, 0, 0]
        elif i == 6:
            src, dst = ha.at[k, 1], hr2.at[k, 1, 1]
        else:
            src, dst = hy.at[k], hz2.at[k]
        dev = at_z(1) if i == 0 else at_z(2) if i == 7 else at_x(to)
        return remote(src, dst, h_s.at[k, i], h_r.at[k, i], dev)

    def za_copy(k, dz):
        mine = ag.at[k, rows(x * 128 + zl * 32, 32)]
        return remote(mine, mine, za_s.at[k, dz - 1], za_r.at[k, dz - 1], at_z(dz))

    def xa_copy(k, i):
        if i < 2:
            part, to = ag.at[k, rows(chunk(x), 128)], (xp, xm)[i]
        elif i == 2:
            part, to = ag.at[k, rows(chunk(xm), 64)], xp
        else:
            part, to = ag.at[k, rows(chunk(xp) + 64, 64)], xm
        return remote(part, part, xa_s.at[k, i], xa_r.at[k, i], at_x(to))

    def ha_copy(k, i):
        if i == 0:
            part, dev = hg.at[k, x, b1, b0], at_z(2)
        elif i == 1:
            part, dev = hg.at[k, x, :, b0], at_x(xp)
        elif i == 2:
            part, dev = hg.at[k, x, :, b0], at_x(xm)
        elif i == 3:
            part, dev = hg.at[k, xm, 0, b0], at_x(xp)
        elif i == 4:
            part, dev = hg.at[k, xp, 1, b0], at_x(xm)
        else:
            part, dev = hg.at[k, :, :, b0], at_z(1)
        return remote(part, part, ha_s.at[k, i], ha_r.at[k, i], dev)

    def out_local(k):
        return (
            pltpu.make_async_copy(go.at[k, feats(c), pl.ds(0, W)], gate_g.at[:, cols(c, k)], ol.at[k, 0]),
            pltpu.make_async_copy(go.at[k, feats(c), pl.ds(W, W)], up_g.at[:, cols(c, k)], ol.at[k, 1]),
            pltpu.make_async_copy(do.at[k, :, feats(c)], down_g.at[cols(c, k), :], ol.at[k, 2]),
        )

    def out_remote(k):
        o = 1 - c
        return (
            remote(go.at[k, feats(o), pl.ds(0, W)], gate_g.at[:, cols(c, k)], os_.at[k, 0], or_.at[k, 0], at_co),
            remote(go.at[k, feats(o), pl.ds(W, W)], up_g.at[:, cols(c, k)], os_.at[k, 1], or_.at[k, 1], at_co),
            remote(do.at[k, :, feats(o)], down_g.at[cols(c, k), :], os_.at[k, 2], or_.at[k, 2], at_co),
        )

    def s0(k):
        for d in w_local(k):
            d.wait()
        for d in w_remote(k):
            d.wait_recv()
        b = k % 5
        p = dot(tc[0], wgu[k], NN)
        s32[b] = p
        sb[k] = p.astype(BF)
        for i in range(4):
            x_copy(k, i).start()
        q = dot(tc[1], wd[k], NT).reshape(4, 2, 2, 32, W)
        h32[b] = q
        hs[k] = q.astype(BF)
        h_copy(k, 0).start()

    def s1(k):
        b = k % 5
        x_copy(k, 0).wait_recv()
        a2[k, 0] = (s32[b, rows(chunk(xp), 64)] + r1[k, 0].astype(F32)).astype(BF)
        x_copy(k, 4).start()
        x_copy(k, 1).wait_recv()
        a2[k, 1] = (s32[b, rows(chunk(xm) + 64, 64)] + r1[k, 1].astype(F32)).astype(BF)
        x_copy(k, 5).start()
        h_copy(k, 0).wait_recv()
        half = h32[b, :, :, b0] + hz1[k].astype(F32)
        h32[b, :, :, b0] = half
        hb[k] = half.astype(BF)
        for i in (1, 2, 3, 4):
            h_copy(k, i).start()

    def s2(k):
        b = k % 5
        for i in (2, 3, 4, 5):
            x_copy(k, i).wait_recv()
        total = s32[b, rows(chunk(x), 128)] + (r2[k, 0].astype(F32) + r2[k, 1].astype(F32))
        s32[b, rows(chunk(x), 128)] = total
        yb[k] = total.astype(BF)
        for dz in (2, 1, 3):
            z_copy(k, dz).start()
        h_copy(k, 1).wait_recv()
        ha[k, 0] = (h32[b, xp, 0, b0] + hr1[k, 0].astype(F32)).astype(BF)
        h_copy(k, 5).start()
        h_copy(k, 2).wait_recv()
        ha[k, 1] = (h32[b, xm, 1, b0] + hr1[k, 1].astype(F32)).astype(BF)
        h_copy(k, 6).start()

    def s3(k):
        b = k % 5
        for i in (3, 4, 5, 6):
            h_copy(k, i).wait_recv()
        total = h32[b, x, :, b0] + (hr2[k, 0].astype(F32) + hr2[k, 1].astype(F32))
        h32[b, x, :, b0] = total
        hy[k] = h32[b, x, 1 - b1, b0].astype(BF)
        h_copy(k, 7).start()

    def s4(k):
        b = k % 5
        for dz in (1, 2, 3):
            z_copy(k, dz).wait_recv()
        total = s32[b, rows(chunk(x) + zl * 32, 32)]
        for i in range(3):
            total = total + zr[k, i].astype(F32)
        g, u = total[:, :W], total[:, W:]
        s = 1.0 / (1.0 + jnp.exp(-g))
        hg[k, x, b1, b0] = (g * s * u).astype(BF)
        ha_copy(k, 0).start()
        h_copy(k, 7).wait_recv()
        grad = h32[b, x, b1, b0] + hz2[k].astype(F32)
        here = rows(x * 128 + zl * 32, 32)
        ag[k, here, :W] = (grad * u * s * (1.0 + g * (1.0 - s))).astype(BF)
        ag[k, here, W:] = (grad * g * s).astype(BF)
        for dz in (2, 1, 3):
            za_copy(k, dz).start()

    def s5(k):
        ha_copy(k, 0).wait_recv()
        ha_copy(k, 1).start()
        ha_copy(k, 2).start()
        for dz in (1, 2, 3):
            za_copy(k, dz).wait_recv()
        xa_copy(k, 0).start()
        xa_copy(k, 1).start()

    def s6(k):
        ha_copy(k, 1).wait_recv()
        ha_copy(k, 3).start()
        ha_copy(k, 2).wait_recv()
        ha_copy(k, 4).start()
        xa_copy(k, 0).wait_recv()
        xa_copy(k, 2).start()
        xa_copy(k, 1).wait_recv()
        xa_copy(k, 3).start()

    def s7(k):
        ha_copy(k, 3).wait_recv()
        ha_copy(k, 4).wait_recv()
        ha_copy(k, 5).start()
        xa_copy(k, 2).wait_recv()
        xa_copy(k, 3).wait_recv()
        go[k] = dot(tc[0], ag[k], TN).astype(BF)
        for d in out_remote(k)[:2]:
            d.start()
        for d in out_local(k)[:2]:
            d.start()
        acc[1] += dot(ag[k], wgu[k], NT)

    def s8(k):
        ha_copy(k, 5).wait_recv()
        h = hg[k].reshape(512, W)
        do[k] = dot(h, tc[1], TN).astype(BF)
        out_remote(k)[2].start()
        out_local(k)[2].start()
        acc[0] += dot(h, wd[k], NN)

    @pl.loop(0, NP + 8)
    def _(t):
        @pl.when(t < NP - AHEAD)
        def _():
            for d in w_remote(t + AHEAD):
                d.start()

        for lag, stage in enumerate((s0, s1, s2, s3, s4, s5, s6, s7, s8)):
            k = t - lag

            @pl.when((k >= 0) & (k < NP))
            def _(k=k, stage=stage):
                stage(k)

    def part(dy):
        return rows(((y + dy) % 4) * 128, 128)

    def e1(dy):
        src, dst = acc.at[:, part(dy), feats(1 - c)], e1b.at[:, part(dy)]
        return remote(src, dst, e1_s.at[dy], e1_r.at[dy], at_co)

    def e2(dy):
        src = e2b.at[:, part(dy)]
        return remote(src, e2r.at[dy - 1], e2_s.at[dy - 1], e2_r.at[dy - 1], at_y(dy))

    def e3():
        return remote(e3b, e3r, e3_s, e3_r, at_zh)

    for dy in (2, 1, 3, 0):
        e1(dy).start()
    for dy in (2, 1, 3):
        e1(dy).wait_recv()
        e2b[:, part(dy)] = (acc[:, part(dy), feats(c)] + e1b[:, part(dy)]).astype(BF)
        e2(dy).start()
    e1(0).wait_recv()
    e1b[:, part(0)] = acc[:, part(0), feats(c)] + e1b[:, part(0)]

    b_zh().wait_send()
    for h in (0, 1):
        for dy in (1, 2, 3):
            b_y(h, dy).wait_send()

    @pl.loop(0, 8)
    def _(j):
        b_co(j).wait_send()

    @pl.loop(0, NP)
    def _(k):
        for d in w_remote(k):
            d.wait_send()
        for i in range(6):
            x_copy(k, i).wait_send()
        for dz in (1, 2, 3):
            z_copy(k, dz).wait_send()
            za_copy(k, dz).wait_send()
        for i in range(4):
            xa_copy(k, i).wait_send()
        for i in range(8):
            h_copy(k, i).wait_send()
        for i in range(6):
            ha_copy(k, i).wait_send()
        for d in out_local(k):
            d.wait()
        for d in out_remote(k):
            d.wait()

    for dy in (1, 2, 3):
        e2(dy).wait_recv()
    there, mine = rows(y * 128 + (1 - zh) * 64, 64), rows(y * 128 + zh * 64, 64)
    rt, rm = rows((1 - zh) * 64, 64), rows(zh * 64, 64)
    away = e1b[:, there]
    for i in range(3):
        away = away + e2r[i, :, rt].astype(F32)
    e3b[...] = away.astype(BF)
    e3().start()
    kept = e1b[:, mine]
    for i in range(3):
        kept = kept + e2r[i, :, rm].astype(F32)
    e3().wait_recv()
    kept = (kept + e3r[...].astype(F32)).astype(BF)
    lo_ref[...] = kept[0]
    tg_ref[...] = kept[1]

    for dy in (0, 1, 2, 3):
        e1(dy).wait_send()
    for dy in (1, 2, 3):
        e2(dy).wait_send()
    e3().wait_send()


def finish(*refs):
    srcs, dsts, stage, ins, outs = refs[:5], refs[5:10], refs[10:15], refs[15], refs[16]
    pairs = []
    for a, b, m in zip(srcs, dsts, stage):
        n = 4 if a.shape[0] > 64 else 1
        step = a.shape[0] // n
        for i in range(n):
            part, k = pl.ds(i * step, step), len(pairs)
            pairs.append(
                (
                    pltpu.make_async_copy(a.at[part], m.at[part], ins.at[k]),
                    pltpu.make_async_copy(m.at[part], b.at[part], outs.at[k]),
                )
            )
    for first, _ in pairs:
        first.start()
    for first, second in pairs:
        first.wait()
        second.start()
    for _, second in pairs:
        second.wait()


def local(tokens, gate_weight, up_weight, down_weight, out_grad):
    def v(*shape, t=BF):
        return pltpu.VMEM(shape, t)

    def sem(*shape):
        return pltpu.SemaphoreType.DMA(shape) if shape else pltpu.SemaphoreType.DMA

    anywhere = pl.BlockSpec(memory_space=pl.ANY)
    vmem = pl.BlockSpec(memory_space=pltpu.VMEM)
    macs = 9 * 512 * 256 * 3584
    shapes = (
        jax.ShapeDtypeStruct((64, 256), BF),
        jax.ShapeDtypeStruct((64, 256), BF),
        jax.ShapeDtypeStruct((256, 3584), BF),
        jax.ShapeDtypeStruct((256, 3584), BF),
        jax.ShapeDtypeStruct((3584, 256), BF),
    )
    results = pl.pallas_call(
        kernel,
        out_shape=shapes,
        in_specs=[anywhere] * 5,
        out_specs=(vmem, vmem, anywhere, anywhere, anywhere),
        scratch_shapes=[
            v(2, 512, 512),
            v(NP, 512, 2 * W),
            v(NP, W, 512),
            v(5, 512, 2 * W, t=F32),
            v(NP, 512, 2 * W),
            v(NP, 2, 64, 2 * W),
            v(NP, 2, 64, 2 * W),
            v(NP, 2, 128, 2 * W),
            v(NP, 128, 2 * W),
            v(NP, 3, 32, 2 * W),
            v(5, 4, 2, 2, 32, W, t=F32),
            v(NP, 4, 2, 2, 32, W),
            v(NP, 4, 2, 32, W),
            v(NP, 4, 2, 32, W),
            v(NP, 2, 32, W),
            v(NP, 2, 32, W),
            v(NP, 2, 2, 32, W),
            v(NP, 32, W),
            v(NP, 32, W),
            v(NP, 512, 2 * W),
            v(NP, 4, 2, 2, 32, W),
            v(NP, 512, 2 * W),
            v(NP, W, 512),
            v(2, 512, 512, t=F32),
            v(2, 512, 256, t=F32),
            v(2, 512, 256),
            v(3, 2, 128, 256),
            v(2, 64, 256),
            v(2, 64, 256),
            sem(2), sem(NP, 3), sem(NP, 3), sem(NP, 3),
            sem(), sem(), sem(2, 3), sem(2, 3), sem(8), sem(8),
            sem(NP, 6), sem(NP, 6), sem(NP, 3), sem(NP, 3),
            sem(NP, 3), sem(NP, 3), sem(NP, 4), sem(NP, 4),
            sem(NP, 8), sem(NP, 8), sem(NP, 6), sem(NP, 6),
            sem(NP, 3), sem(NP, 3), sem(NP, 3),
            sem(4), sem(4), sem(3), sem(3), sem(), sem(),
        ],
        compiler_params=pltpu.CompilerParams(
            collective_id=0, has_side_effects=True, vmem_limit_bytes=60 * 2**20
        ),
        cost_estimate=pl.CostEstimate(flops=2 * macs, bytes_accessed=12 * 2**20, transcendentals=2**16),
        name="swiglu",
    )(tokens, gate_weight, up_weight, down_weight, out_grad)
    return pl.pallas_call(
        finish,
        out_shape=shapes,
        in_specs=[anywhere] * 5,
        out_specs=(anywhere,) * 5,
        scratch_shapes=[v(*a.shape) for a in shapes] + [sem(14), sem(14)],
        compiler_params=pltpu.CompilerParams(vmem_limit_bytes=60 * 2**20),
        cost_estimate=pl.CostEstimate(flops=0, bytes_accessed=12 * 2**20, transcendentals=0),
        name="finish",
    )(*results)


def solution(mesh):
    tokens, weights = P("col", "row"), P("row", "col")
    return jax.shard_map(
        local,
        mesh=mesh,
        in_specs=(tokens, weights, weights, tokens, tokens),
        out_specs=(tokens, tokens, weights, weights, tokens),
        check_vma=False,
    )
```

```python
import jax
import jax.numpy as jnp
from jax import lax
from jax.experimental import pallas as pl
from jax.experimental.pallas import tpu as pltpu
from jax.sharding import PartitionSpec as P

MESH = pl.DeviceIdType.MESH
BF = jnp.bfloat16
F32 = jnp.float32
NP = 7
W = 256
STARTS = (0, 1, 2, 3, 4, 5, 6)
AHEAD = 2
EARLY = 4
HALF = NP * W
F = 256


def dot(a, b, dims):
    return lax.dot_general(a, b, (dims, ((), ())), preferred_element_type=F32)


NN = ((1,), (0,))
NT = ((1,), (1,))
TN = ((0,), (0,))


def kernel(
    tok, gate_w, up_w, down_w, cot,
    lo_ref, tg_ref, gate_g, up_g, down_g,
    tc, wgu, wd, s32, sb, r1, a2, r2, yb, zr1, yc, zr2,
    h32, hs, hz1, hb, hr1, ha, hr2, hy, hz2, ag, hg, go, do, acc, e1b, e2b, e2r, e3b, e3r,
    in_l, wl, ws, wr, zh_s, zh_r, y_s, y_r, co_s, co_r,
    x_s, x_r, z_s, z_r, za_s, za_r, xa_s, xa_r, h_s, h_r, ha_s, ha_r, ol, os_, or_,
    e1_s, e1_r, e2_s, e2_r, e3_s, e3_r,
):
    row, col = lax.axis_index("row"), lax.axis_index("col")
    x, zl, c = row // 8, (row // 2) % 4, row % 2
    y, zh = col // 2, col % 2
    xp, xm, x2 = (x + 1) % 4, (x + 3) % 4, (x + 2) % 4

    def at_x(px):
        return (px * 8 + zl * 2 + c, col)

    def z_of(dz):
        b = (zl % 2) if dz % 2 == 0 else 1 - zl % 2
        h = (zl // 2) if dz < 2 else 1 - zl // 2
        return h * 2 + b

    def at_z(dz):
        return (x * 8 + z_of(dz) * 2 + c, col)

    def at_y(dy):
        return (row, ((y + dy) % 4) * 2 + zh)

    at_co = (x * 8 + zl * 2 + 1 - c, col)
    at_zh = (row, y * 2 + 1 - zh)
    peers = [at_co, at_zh, at_x(xp), at_x(xm)]
    peers += [at_z(d) for d in (1, 2)] + [at_y(d) for d in (1, 2, 3)]

    def remote(src, dst, ss, rs, dev):
        return pltpu.make_async_remote_copy(
            src_ref=src, dst_ref=dst, send_sem=ss, recv_sem=rs, device_id=dev, device_id_type=MESH
        )

    def cols(core, k):
        return pl.ds(pl.multiple_of(core * HALF + k * W, W), W)

    def feats(core):
        return pl.ds(pl.multiple_of(core * F, F), F)

    def rows(start, size):
        return pl.ds(pl.multiple_of(start, size), size)

    def w_local(k):
        return (
            pltpu.make_async_copy(gate_w.at[:, cols(c, k)], wgu.at[k, feats(c), pl.ds(0, W)], wl.at[k, 0]),
            pltpu.make_async_copy(up_w.at[:, cols(c, k)], wgu.at[k, feats(c), pl.ds(W, W)], wl.at[k, 1]),
            pltpu.make_async_copy(down_w.at[cols(c, k), :], wd.at[k, :, feats(c)], wl.at[k, 2]),
        )

    def w_remote(k):
        o = 1 - c
        return (
            remote(gate_w.at[:, cols(o, k)], wgu.at[k, feats(c), pl.ds(0, W)], ws.at[k, 0], wr.at[k, 0], at_co),
            remote(up_w.at[:, cols(o, k)], wgu.at[k, feats(c), pl.ds(W, W)], ws.at[k, 1], wr.at[k, 1], at_co),
            remote(down_w.at[cols(o, k), :], wd.at[k, :, feats(c)], ws.at[k, 2], wr.at[k, 2], at_co),
        )

    def block(j):
        return tc.at[:, j // 2, j % 2, :, feats(c)]

    def b_zh():
        return remote(block(col), block(col), zh_s, zh_r, at_zh)

    def b_y(h, dy):
        b = block(y * 2 + (zh if h == 0 else 1 - zh))
        return remote(b, b, y_s.at[h, dy - 1], y_r.at[h, dy - 1], at_y(dy))

    def b_co(j):
        return remote(block(j), block(j), co_s.at[j], co_r.at[j], at_co)

    ins = (
        pltpu.make_async_copy(tok, tc.at[0, y, zh, :, feats(c)], in_l.at[0]),
        pltpu.make_async_copy(cot, tc.at[1, y, zh, :, feats(c)], in_l.at[1]),
    )
    for d in ins:
        d.start()
    barrier = pltpu.get_barrier_semaphore()
    for p in peers:
        pl.semaphore_signal(barrier, inc=1, device_id=p, device_id_type=MESH)

    @pl.loop(0, NP)
    def _(k):
        for d in w_local(k):
            d.start()

    pl.semaphore_wait(barrier, len(peers))

    for d in ins:
        d.wait()
    b_zh().start()
    for dy in (1, 3, 2):
        b_y(0, dy).start()
    b_co(col).start()
    for k in range(AHEAD):
        for d in w_remote(k):
            d.start()

    b0, b1 = zl % 2, zl // 2

    def x_copy(k, i):
        if i == 0:
            src, dst, to = sb.at[k, x2, 0], r1.at[k, 0], xp
        elif i == 1:
            src, dst, to = sb.at[k, x2, 1], r1.at[k, 1], xm
        elif i == 2:
            src, dst, to = sb.at[k, xp, 1], r2.at[k, 0, 1], xp
        elif i == 3:
            src, dst, to = sb.at[k, xm, 0], r2.at[k, 1, 0], xm
        elif i == 4:
            src, dst, to = a2.at[k, 0], r2.at[k, 0, 0], xp
        else:
            src, dst, to = a2.at[k, 1], r2.at[k, 1, 1], xm
        return remote(src, dst, x_s.at[k, i], x_r.at[k, i], at_x(to))

    def z_copy(k, i):
        if i == 0:
            return remote(yb.at[k, :, 1 - b0], zr1.at[k], z_s.at[k, 0], z_r.at[k, 0], at_z(1))
        return remote(yc.at[k], zr2.at[k], z_s.at[k, 1], z_r.at[k, 1], at_z(2))

    def h_copy(k, i):
        to = xp if i in (1, 3, 5) else xm
        if i in (0, 8):
            src, dst = hs.at[k, :, i // 8, 1 - b0], hz1.at[k, :, i // 8]
        elif i == 1:
            src, dst = hb.at[k, x2, 0], hr1.at[k, 0]
        elif i == 2:
            src, dst = hb.at[k, x2, 1], hr1.at[k, 1]
        elif i == 3:
            src, dst = hb.at[k, xp, 1], hr2.at[k, 0, 1]
        elif i == 4:
            src, dst = hb.at[k, xm, 0], hr2.at[k, 1, 0]
        elif i == 5:
            src, dst = ha.at[k, 0], hr2.at[k, 0, 0]
        elif i == 6:
            src, dst = ha.at[k, 1], hr2.at[k, 1, 1]
        else:
            src, dst = hy.at[k], hz2.at[k]
        dev = at_z(1) if i in (0, 8) else at_z(2) if i == 7 else at_x(to)
        return remote(src, dst, h_s.at[k, i], h_r.at[k, i], dev)

    def za_copy(k, i):
        part, dev = (ag.at[k, x, b1, b0], at_z(2)) if i == 0 else (ag.at[k, x, :, b0], at_z(1))
        return remote(part, part, za_s.at[k, i], za_r.at[k, i], dev)

    def xa_copy(k, i):
        part = ag.at[k, x] if i < 2 else ag.at[k, xm, 0] if i == 2 else ag.at[k, xp, 1]
        return remote(part, part, xa_s.at[k, i], xa_r.at[k, i], at_x(xm if i % 2 else xp))

    def ha_copy(k, i):
        if i == 0:
            part, dev = hg.at[k, x, b1, b0], at_z(2)
        elif i == 1:
            part, dev = hg.at[k, x, :, b0], at_x(xp)
        elif i == 2:
            part, dev = hg.at[k, x, :, b0], at_x(xm)
        elif i == 3:
            part, dev = hg.at[k, xm, 0, b0], at_x(xp)
        elif i == 4:
            part, dev = hg.at[k, xp, 1, b0], at_x(xm)
        else:
            part, dev = hg.at[k, :, :, b0], at_z(1)
        return remote(part, part, ha_s.at[k, i], ha_r.at[k, i], dev)

    def out_refs(k, i, core):
        if i == 2:
            return do.at[k, :, feats(core)], down_g.at[cols(c, k), :]
        return go.at[k, feats(core), pl.ds(i * W, W)], (gate_g, up_g)[i].at[:, cols(c, k)]

    def out_local(k, i):
        return pltpu.make_async_copy(*out_refs(k, i, c), ol.at[k, i])

    def out_remote(k, i):
        return remote(*out_refs(k, i, 1 - c), os_.at[k, i], or_.at[k, i], at_co)

    def weights_here(k):
        for d in w_local(k):
            d.wait()
        for d in w_remote(k):
            d.wait_recv()

    def half(k, b):
        p = dot(tc[0, :, b].reshape(256, 512), wgu[k], NN).reshape(4, 64, 2 * W)
        s32[k, :, b] = p
        sb[k, :, b] = p.astype(BF)
        q = dot(tc[1, :, b].reshape(256, 512), wd[k], NT).reshape(4, 2, 32, W)
        h32[k, :, b] = q
        hs[k, :, b] = q.astype(BF)
        for which, sends in ((0, (0, 3, 0)), (1, (1, 2, 8))):

            @pl.when(b == which)
            def _(sends=sends):
                x_copy(k, sends[0]).start()
                x_copy(k, sends[1]).start()
                h_copy(k, sends[2]).start()

    def s0(k):
        @pl.when(k >= EARLY)
        def _():
            weights_here(k)
            half(k, zh)

        half(k, 1 - zh)

    def s1(k):
        x_copy(k, 0).wait_recv()
        a2[k, 0] = (s32[k, xp, 0] + r1[k, 0].astype(F32)).astype(BF)
        x_copy(k, 4).start()
        x_copy(k, 1).wait_recv()
        a2[k, 1] = (s32[k, xm, 1] + r1[k, 1].astype(F32)).astype(BF)
        x_copy(k, 5).start()
        h_copy(k, 0).wait_recv()
        h_copy(k, 8).wait_recv()
        half = h32[k, :, :, b0] + hz1[k].astype(F32)
        h32[k, :, :, b0] = half
        hb[k] = half.astype(BF)
        for i in (1, 2, 3, 4):
            h_copy(k, i).start()

    def s2(k):
        for i in (2, 3, 4, 5):
            x_copy(k, i).wait_recv()
        total = s32[k, x] + (r2[k, 0].astype(F32) + r2[k, 1].astype(F32))
        s32[k, x] = total
        yb[k] = total.astype(BF).reshape(2, 2, 32, 2 * W)
        z_copy(k, 0).start()
        h_copy(k, 1).wait_recv()
        ha[k, 0] = (h32[k, xp, 0, b0] + hr1[k, 0].astype(F32)).astype(BF)
        h_copy(k, 5).start()
        h_copy(k, 2).wait_recv()
        ha[k, 1] = (h32[k, xm, 1, b0] + hr1[k, 1].astype(F32)).astype(BF)
        h_copy(k, 6).start()

    def s3(k):
        z_copy(k, 0).wait_recv()
        mine = rows(b0 * 32, 32)
        yc[k] = (s32[k, x, 1 - b1, mine] + zr1[k, 1 - b1].astype(F32)).astype(BF)
        z_copy(k, 1).start()
        s32[k, x, b1, mine] = s32[k, x, b1, mine] + zr1[k, b1].astype(F32)
        for i in (3, 4, 5, 6):
            h_copy(k, i).wait_recv()
        total = h32[k, x, :, b0] + (hr2[k, 0].astype(F32) + hr2[k, 1].astype(F32))
        h32[k, x, :, b0] = total
        hy[k] = h32[k, x, 1 - b1, b0].astype(BF)
        h_copy(k, 7).start()

    def s4(k):
        z_copy(k, 1).wait_recv()
        total = s32[k, x, b1, rows(b0 * 32, 32)] + zr2[k].astype(F32)
        g, u = total[:, :W], total[:, W:]
        s = 1.0 / (1.0 + jnp.exp(-g))
        hg[k, x, b1, b0] = (g * s * u).astype(BF)
        ha_copy(k, 0).start()
        h_copy(k, 7).wait_recv()
        grad = h32[k, x, b1, b0] + hz2[k].astype(F32)
        ag[k, x, b1, b0, :, :W] = (grad * u * s * (1.0 + g * (1.0 - s))).astype(BF)
        ag[k, x, b1, b0, :, W:] = (grad * g * s).astype(BF)
        za_copy(k, 0).start()

    def s5(k):
        za_copy(k, 0).wait_recv()
        za_copy(k, 1).start()
        ha_copy(k, 0).wait_recv()
        ha_copy(k, 1).start()
        ha_copy(k, 2).start()

    def s6(k):
        za_copy(k, 1).wait_recv()
        xa_copy(k, 0).start()
        xa_copy(k, 1).start()
        ha_copy(k, 1).wait_recv()
        ha_copy(k, 3).start()
        ha_copy(k, 2).wait_recv()
        ha_copy(k, 4).start()

    def s7(k):
        xa_copy(k, 0).wait_recv()
        xa_copy(k, 2).start()
        xa_copy(k, 1).wait_recv()
        xa_copy(k, 3).start()
        ha_copy(k, 3).wait_recv()
        ha_copy(k, 4).wait_recv()
        ha_copy(k, 5).start()

    def deltas(k):
        return ag[k].reshape(512, 2 * W)

    def hidden(k):
        return hg[k].reshape(512, W)

    def add_token_grad(k):
        xa_copy(k, 2).wait_recv()
        xa_copy(k, 3).wait_recv()
        acc[1] += dot(deltas(k), wgu[k], NT)

    def add_layer_out(k):
        ha_copy(k, 5).wait_recv()
        acc[0] += dot(hidden(k), wd[k], NN)

    def weight_grads(k):
        go[k] = dot(tc[0].reshape(512, 512), deltas(k), TN).astype(BF)
        for i in range(2):
            out_remote(k, i).start()
            out_local(k, i).start()
        do[k] = dot(hidden(k), tc[1].reshape(512, 512), TN).astype(BF)
        out_remote(k, 2).start()
        out_local(k, 2).start()

    def s8(k):
        add_token_grad(k)
        add_layer_out(k)
        weight_grads(k)

    def forward(h):
        for dy in (1, 3, 2):
            b_y(h, dy).wait_recv()
            b_co(((y + 4 - dy) % 4) * 2 + (zh if h == 0 else 1 - zh)).start()

    def early(k):
        weights_here(k)
        half(k, zh)

    b_zh().wait_recv()
    for dy in (1, 2, 3):
        b_y(1, dy).start()
    forward(0)
    b_co(y * 2 + 1 - zh).start()

    @pl.loop(AHEAD, EARLY + 1)
    def _(k):
        for d in w_remote(k):
            d.start()

    acc[...] = jnp.zeros_like(acc)
    for p in range(4):
        b_co(p * 2 + zh).wait_recv()
    pl.loop(0, EARLY // 2)(early)
    forward(1)
    pl.loop(EARLY // 2, EARLY)(early)
    for p in range(4):
        b_co(p * 2 + 1 - zh).wait_recv()

    def begun(slot):
        return sum((slot + 63 - start) // 64 for start in STARTS)

    @pl.loop(0, STARTS[-1] + 9)
    def _(t):
        @pl.when(t < NP - EARLY - 1)
        def _():
            for d in w_remote(t + EARLY + 1):
                d.start()

        for lag, stage in ((0, s0), (2, s1), (3, s2), (4, s3), (5, s4), (6, s5), (7, s6), (8, s7), (9, s8)):

            @pl.loop(begun(t - lag), begun(t - lag + 1))
            def _(k, stage=stage):
                stage(k)

    def part(dy):
        return rows(((y + dy) % 4) * 128, 128)

    def e1(i, dy):
        src, dst = acc.at[i, part(dy), feats(1 - c)], e1b.at[i, part(dy)]
        return remote(src, dst, e1_s.at[i, dy], e1_r.at[i, dy], at_co)

    def e2(i, dy):
        src, n = e2b.at[i, part(dy)], dy - 1
        return remote(src, e2r.at[n, i], e2_s.at[i, n], e2_r.at[i, n], at_y(dy))

    def e3(i):
        return remote(e3b.at[i], e3r.at[i], e3_s.at[i], e3_r.at[i], at_zh)

    add_token_grad(NP - 1)
    for dy in (2, 1, 3, 0):
        e1(1, dy).start()
    add_layer_out(NP - 1)
    for dy in (2, 1, 3, 0):
        e1(0, dy).start()
    for i in (1, 0):
        for dy in (2, 1, 3):
            e1(i, dy).wait_recv()
            e2b[i, part(dy)] = (acc[i, part(dy), feats(c)] + e1b[i, part(dy)]).astype(BF)
            e2(i, dy).start()
    weight_grads(NP - 1)
    for i in (1, 0):
        e1(i, 0).wait_recv()
        e1b[i, part(0)] = acc[i, part(0), feats(c)] + e1b[i, part(0)]
    there, mine = rows(y * 128 + (1 - zh) * 64, 64), rows(y * 128 + zh * 64, 64)
    rt, rm = rows((1 - zh) * 64, 64), rows(zh * 64, 64)
    for i in (1, 0):
        for dy in (1, 3, 2):
            e2(i, dy).wait_recv()
        away = e1b[i, there]
        for n in range(3):
            away = away + e2r[n, i, rt].astype(F32)
        e3b[i] = away.astype(BF)
        e3(i).start()

    b_zh().wait_send()
    for h in (0, 1):
        for dy in (1, 2, 3):
            b_y(h, dy).wait_send()

    @pl.loop(0, 8)
    def _(j):
        b_co(j).wait_send()

    @pl.loop(0, NP)
    def _(k):
        for d in w_remote(k):
            d.wait_send()
        for i in range(6):
            x_copy(k, i).wait_send()
        for i in range(2):
            z_copy(k, i).wait_send()
            za_copy(k, i).wait_send()
        for i in range(4):
            xa_copy(k, i).wait_send()
        for i in range(9):
            h_copy(k, i).wait_send()
        for i in range(6):
            ha_copy(k, i).wait_send()
        for i in range(3):
            out_local(k, i).wait()
            out_remote(k, i).wait()

    for i, out in ((1, tg_ref), (0, lo_ref)):
        kept = e1b[i, mine]
        for n in range(3):
            kept = kept + e2r[n, i, rm].astype(F32)
        e3(i).wait_recv()
        out[...] = (kept + e3r[i].astype(F32)).astype(BF)

    for i in (0, 1):
        for dy in (0, 1, 2, 3):
            e1(i, dy).wait_send()
        for dy in (1, 2, 3):
            e2(i, dy).wait_send()
        e3(i).wait_send()


def finish(*refs):
    srcs, dsts, stage, ins, outs = refs[:5], refs[5:10], refs[10:15], refs[15], refs[16]
    pairs = []
    for a, b, m in zip(srcs, dsts, stage):
        n = 4 if a.shape[0] > 64 else 1
        step = a.shape[0] // n
        for i in range(n):
            part, k = pl.ds(i * step, step), len(pairs)
            pairs.append(
                (
                    pltpu.make_async_copy(a.at[part], m.at[part], ins.at[k]),
                    pltpu.make_async_copy(m.at[part], b.at[part], outs.at[k]),
                )
            )
    for first, _ in pairs:
        first.start()
    for first, second in pairs:
        first.wait()
        second.start()
    for _, second in pairs:
        second.wait()


def local(tokens, gate_weight, up_weight, down_weight, out_grad):
    def v(*shape, t=BF):
        return pltpu.VMEM(shape, t)

    def sem(*shape):
        return pltpu.SemaphoreType.DMA(shape) if shape else pltpu.SemaphoreType.DMA

    anywhere = pl.BlockSpec(memory_space=pl.ANY)
    vmem = pl.BlockSpec(memory_space=pltpu.VMEM)
    macs = 9 * 512 * 256 * 3584
    shapes = (
        jax.ShapeDtypeStruct((64, 256), BF),
        jax.ShapeDtypeStruct((64, 256), BF),
        jax.ShapeDtypeStruct((256, 3584), BF),
        jax.ShapeDtypeStruct((256, 3584), BF),
        jax.ShapeDtypeStruct((3584, 256), BF),
    )
    results = pl.pallas_call(
        kernel,
        out_shape=shapes,
        in_specs=[anywhere] * 5,
        out_specs=(vmem, vmem, anywhere, anywhere, anywhere),
        scratch_shapes=[
            v(2, 4, 2, 64, 512),
            v(NP, 512, 2 * W),
            v(NP, W, 512),
            v(NP, 4, 2, 64, 2 * W, t=F32),
            v(NP, 4, 2, 64, 2 * W),
            v(NP, 2, 64, 2 * W),
            v(NP, 2, 64, 2 * W),
            v(NP, 2, 2, 64, 2 * W),
            v(NP, 2, 2, 32, 2 * W),
            v(NP, 2, 32, 2 * W),
            v(NP, 32, 2 * W),
            v(NP, 32, 2 * W),
            v(NP, 4, 2, 2, 32, W, t=F32),
            v(NP, 4, 2, 2, 32, W),
            v(NP, 4, 2, 32, W),
            v(NP, 4, 2, 32, W),
            v(NP, 2, 32, W),
            v(NP, 2, 32, W),
            v(NP, 2, 2, 32, W),
            v(NP, 32, W),
            v(NP, 32, W),
            v(NP, 4, 2, 2, 32, 2 * W),
            v(NP, 4, 2, 2, 32, W),
            v(NP, 512, 2 * W),
            v(NP, W, 512),
            v(2, 512, 512, t=F32),
            v(2, 512, 256, t=F32),
            v(2, 512, 256),
            v(3, 2, 128, 256),
            v(2, 64, 256),
            v(2, 64, 256),
            sem(2), sem(NP, 3), sem(NP, 3), sem(NP, 3),
            sem(), sem(), sem(2, 3), sem(2, 3), sem(8), sem(8),
            sem(NP, 6), sem(NP, 6), sem(NP, 2), sem(NP, 2),
            sem(NP, 2), sem(NP, 2), sem(NP, 4), sem(NP, 4),
            sem(NP, 9), sem(NP, 9), sem(NP, 6), sem(NP, 6),
            sem(NP, 3), sem(NP, 3), sem(NP, 3),
            sem(2, 4), sem(2, 4), sem(2, 3), sem(2, 3), sem(2), sem(2),
        ],
        compiler_params=pltpu.CompilerParams(
            collective_id=0, has_side_effects=True, vmem_limit_bytes=60 * 2**20
        ),
        cost_estimate=pl.CostEstimate(flops=2 * macs, bytes_accessed=12 * 2**20, transcendentals=2**16),
        name="swiglu",
    )(tokens, gate_weight, up_weight, down_weight, out_grad)
    return pl.pallas_call(
        finish,
        out_shape=shapes,
        in_specs=[anywhere] * 5,
        out_specs=(anywhere,) * 5,
        scratch_shapes=[v(*a.shape) for a in shapes] + [sem(14), sem(14)],
        compiler_params=pltpu.CompilerParams(vmem_limit_bytes=60 * 2**20),
        cost_estimate=pl.CostEstimate(flops=0, bytes_accessed=12 * 2**20, transcendentals=0),
        name="finish",
    )(*results)


def solution(mesh):
    tokens, weights = P("col", "row"), P("row", "col")
    return jax.shard_map(
        local,
        mesh=mesh,
        in_specs=(tokens, weights, weights, tokens, tokens),
        out_specs=(tokens, tokens, weights, weights, tokens),
        check_vma=False,
    )
```

```python
import jax
import jax.numpy as jnp
from jax import lax
from jax.experimental import pallas as pl
from jax.experimental.pallas import tpu as pltpu
from jax.sharding import PartitionSpec as P

MESH = pl.DeviceIdType.MESH
BF = jnp.bfloat16
F32 = jnp.float32
NP = 7
W = 256
AHEAD = 2
EARLY = 4
HALF = NP * W
F = 256


def dot(a, b, dims):
    return lax.dot_general(a, b, (dims, ((), ())), preferred_element_type=F32)


NN = ((1,), (0,))
NT = ((1,), (1,))
TN = ((0,), (0,))


def kernel(
    tok, gate_w, up_w, down_w, cot,
    lo_ref, tg_ref, gate_g, up_g, down_g,
    tc, wgu, wd, s32, sb, r1, a2, r2, yb, zr1, yc, zr2,
    h32, hs, hz1, hb, hr1, ha, hr2, hy, hz2, ag, hg, go, do, acc, e1b, e2b, e2r, e3b, e3r,
    in_l, wl, ws, wr, zh_s, zh_r, y_s, y_r, co_s, co_r,
    x_s, x_r, z_s, z_r, za_s, za_r, xa_s, xa_r, h_s, h_r, ha_s, ha_r, ol, os_, or_,
    e1_s, e1_r, e2_s, e2_r, e3_s, e3_r,
):
    row, col = lax.axis_index("row"), lax.axis_index("col")
    x, zl, c = row // 8, (row // 2) % 4, row % 2
    y, zh = col // 2, col % 2
    xp, xm, x2 = (x + 1) % 4, (x + 3) % 4, (x + 2) % 4

    def at_x(px):
        return (px * 8 + zl * 2 + c, col)

    def z_of(dz):
        b = (zl % 2) if dz % 2 == 0 else 1 - zl % 2
        h = (zl // 2) if dz < 2 else 1 - zl // 2
        return h * 2 + b

    def at_z(dz):
        return (x * 8 + z_of(dz) * 2 + c, col)

    def at_y(dy):
        return (row, ((y + dy) % 4) * 2 + zh)

    at_co = (x * 8 + zl * 2 + 1 - c, col)
    at_zh = (row, y * 2 + 1 - zh)
    peers = [at_co, at_zh, at_x(xp), at_x(xm)]
    peers += [at_z(d) for d in (1, 2, 3)] + [at_y(d) for d in (1, 2, 3)]

    def remote(src, dst, ss, rs, dev):
        return pltpu.make_async_remote_copy(
            src_ref=src, dst_ref=dst, send_sem=ss, recv_sem=rs, device_id=dev, device_id_type=MESH
        )

    def cols(core, k):
        return pl.ds(pl.multiple_of(core * HALF + k * W, W), W)

    def feats(core):
        return pl.ds(pl.multiple_of(core * F, F), F)

    def rows(start, size):
        return pl.ds(pl.multiple_of(start, size), size)

    def w_local(k):
        return (
            pltpu.make_async_copy(gate_w.at[:, cols(c, k)], wgu.at[k, feats(c), pl.ds(0, W)], wl.at[k, 0]),
            pltpu.make_async_copy(up_w.at[:, cols(c, k)], wgu.at[k, feats(c), pl.ds(W, W)], wl.at[k, 1]),
            pltpu.make_async_copy(down_w.at[cols(c, k), :], wd.at[k, :, feats(c)], wl.at[k, 2]),
        )

    def w_remote(k):
        o = 1 - c
        return (
            remote(gate_w.at[:, cols(o, k)], wgu.at[k, feats(c), pl.ds(0, W)], ws.at[k, 0], wr.at[k, 0], at_co),
            remote(up_w.at[:, cols(o, k)], wgu.at[k, feats(c), pl.ds(W, W)], ws.at[k, 1], wr.at[k, 1], at_co),
            remote(down_w.at[cols(o, k), :], wd.at[k, :, feats(c)], ws.at[k, 2], wr.at[k, 2], at_co),
        )

    def block(j):
        return tc.at[:, j // 2, j % 2, :, feats(c)]

    def b_zh():
        return remote(block(col), block(col), zh_s, zh_r, at_zh)

    def b_y(h, dy):
        b = block(y * 2 + (zh if h == 0 else 1 - zh))
        return remote(b, b, y_s.at[h, dy - 1], y_r.at[h, dy - 1], at_y(dy))

    def b_co(j):
        return remote(block(j), block(j), co_s.at[j], co_r.at[j], at_co)

    ins = (
        pltpu.make_async_copy(tok, tc.at[0, y, zh, :, feats(c)], in_l.at[0]),
        pltpu.make_async_copy(cot, tc.at[1, y, zh, :, feats(c)], in_l.at[1]),
    )
    for d in ins:
        d.start()
    barrier = pltpu.get_barrier_semaphore()
    for p in peers:
        pl.semaphore_signal(barrier, inc=1, device_id=p, device_id_type=MESH)

    @pl.loop(0, NP)
    def _(k):
        for d in w_local(k):
            d.start()

    pl.semaphore_wait(barrier, len(peers))

    for d in ins:
        d.wait()
    b_zh().start()
    for dy in (1, 3, 2):
        b_y(0, dy).start()
    b_co(col).start()
    for k in range(AHEAD):
        for d in w_remote(k):
            d.start()

    b0, b1 = zl % 2, zl // 2

    def x_copy(k, i):
        if i == 0:
            src, dst, to = sb.at[k, x2, 0], r1.at[k, 0], xp
        elif i == 1:
            src, dst, to = sb.at[k, x2, 1], r1.at[k, 1], xm
        elif i == 2:
            src, dst, to = sb.at[k, xp, 1], r2.at[k, 0, 1], xp
        elif i == 3:
            src, dst, to = sb.at[k, xm, 0], r2.at[k, 1, 0], xm
        elif i == 4:
            src, dst, to = a2.at[k, 0], r2.at[k, 0, 0], xp
        else:
            src, dst, to = a2.at[k, 1], r2.at[k, 1, 1], xm
        return remote(src, dst, x_s.at[k, i], x_r.at[k, i], at_x(to))

    def z_copy(k, i):
        if i == 0:
            return remote(yb.at[k, :, 1 - b0], zr1.at[k], z_s.at[k, 0], z_r.at[k, 0], at_z(1))
        return remote(yc.at[k], zr2.at[k], z_s.at[k, 1], z_r.at[k, 1], at_z(2))

    def h_copy(k, i):
        to = xp if i in (1, 3, 5) else xm
        if i in (0, 8):
            src, dst = hs.at[k, :, i // 8, 1 - b0], hz1.at[k, :, i // 8]
        elif i == 1:
            src, dst = hb.at[k, x2, 0], hr1.at[k, 0]
        elif i == 2:
            src, dst = hb.at[k, x2, 1], hr1.at[k, 1]
        elif i == 3:
            src, dst = hb.at[k, xp, 1], hr2.at[k, 0, 1]
        elif i == 4:
            src, dst = hb.at[k, xm, 0], hr2.at[k, 1, 0]
        elif i == 5:
            src, dst = ha.at[k, 0], hr2.at[k, 0, 0]
        elif i == 6:
            src, dst = ha.at[k, 1], hr2.at[k, 1, 1]
        else:
            src, dst = hy.at[k], hz2.at[k]
        dev = at_z(1) if i in (0, 8) else at_z(2) if i == 7 else at_x(to)
        return remote(src, dst, h_s.at[k, i], h_r.at[k, i], dev)

    def za_copy(k, dz):
        part = ag.at[k, x, b1, b0]
        return remote(part, part, za_s.at[k, dz - 1], za_r.at[k, dz - 1], at_z(dz))

    def xa_copy(k, i):
        part = ag.at[k, x] if i < 2 else ag.at[k, xm, 0] if i == 2 else ag.at[k, xp, 1]
        return remote(part, part, xa_s.at[k, i], xa_r.at[k, i], at_x(xm if i % 2 else xp))

    def ha_copy(k, i):
        if i == 0:
            part, dev = hg.at[k, x, b1, b0], at_z(2)
        elif i == 1:
            part, dev = hg.at[k, x, :, b0], at_x(xp)
        elif i == 2:
            part, dev = hg.at[k, x, :, b0], at_x(xm)
        elif i == 3:
            part, dev = hg.at[k, xm, 0, b0], at_x(xp)
        elif i == 4:
            part, dev = hg.at[k, xp, 1, b0], at_x(xm)
        else:
            part, dev = hg.at[k, :, :, b0], at_z(1)
        return remote(part, part, ha_s.at[k, i], ha_r.at[k, i], dev)

    def out_refs(k, i, core):
        if i == 2:
            return do.at[k, :, feats(core)], down_g.at[cols(c, k), :]
        return go.at[k, feats(core), pl.ds(i * W, W)], (gate_g, up_g)[i].at[:, cols(c, k)]

    def out_local(k, i):
        return pltpu.make_async_copy(*out_refs(k, i, c), ol.at[k, i])

    def out_remote(k, i):
        return remote(*out_refs(k, i, 1 - c), os_.at[k, i], or_.at[k, i], at_co)

    def weights_here(k):
        for d in w_local(k):
            d.wait()
        for d in w_remote(k):
            d.wait_recv()

    def half(k, b):
        p = dot(tc[0, :, b].reshape(256, 512), wgu[k], NN).reshape(4, 64, 2 * W)
        s32[k, :, b] = p
        sb[k, :, b] = p.astype(BF)
        q = dot(tc[1, :, b].reshape(256, 512), wd[k], NT).reshape(4, 2, 32, W)
        h32[k, :, b] = q
        hs[k, :, b] = q.astype(BF)
        for which, sends in ((0, (0, 3, 0)), (1, (1, 2, 8))):

            @pl.when(b == which)
            def _(sends=sends):
                x_copy(k, sends[0]).start()
                x_copy(k, sends[1]).start()
                h_copy(k, sends[2]).start()

    def s0(k):
        @pl.when(k >= EARLY)
        def _():
            weights_here(k)
            half(k, zh)

        half(k, 1 - zh)

    def s1(k):
        x_copy(k, 0).wait_recv()
        a2[k, 0] = (s32[k, xp, 0] + r1[k, 0].astype(F32)).astype(BF)
        x_copy(k, 4).start()
        x_copy(k, 1).wait_recv()
        a2[k, 1] = (s32[k, xm, 1] + r1[k, 1].astype(F32)).astype(BF)
        x_copy(k, 5).start()
        h_copy(k, 0).wait_recv()
        h_copy(k, 8).wait_recv()
        half = h32[k, :, :, b0] + hz1[k].astype(F32)
        h32[k, :, :, b0] = half
        hb[k] = half.astype(BF)
        for i in (1, 2, 3, 4):
            h_copy(k, i).start()

    def s2(k):
        for i in (2, 3, 4, 5):
            x_copy(k, i).wait_recv()
        total = s32[k, x] + (r2[k, 0].astype(F32) + r2[k, 1].astype(F32))
        s32[k, x] = total
        yb[k] = total.astype(BF).reshape(2, 2, 32, 2 * W)
        z_copy(k, 0).start()
        h_copy(k, 1).wait_recv()
        ha[k, 0] = (h32[k, xp, 0, b0] + hr1[k, 0].astype(F32)).astype(BF)
        h_copy(k, 5).start()
        h_copy(k, 2).wait_recv()
        ha[k, 1] = (h32[k, xm, 1, b0] + hr1[k, 1].astype(F32)).astype(BF)
        h_copy(k, 6).start()

    def s3(k):
        z_copy(k, 0).wait_recv()
        mine = rows(b0 * 32, 32)
        yc[k] = (s32[k, x, 1 - b1, mine] + zr1[k, 1 - b1].astype(F32)).astype(BF)
        z_copy(k, 1).start()
        s32[k, x, b1, mine] = s32[k, x, b1, mine] + zr1[k, b1].astype(F32)
        for i in (3, 4, 5, 6):
            h_copy(k, i).wait_recv()
        total = h32[k, x, :, b0] + (hr2[k, 0].astype(F32) + hr2[k, 1].astype(F32))
        h32[k, x, :, b0] = total
        hy[k] = h32[k, x, 1 - b1, b0].astype(BF)
        h_copy(k, 7).start()

    def s4(k):
        z_copy(k, 1).wait_recv()
        total = s32[k, x, b1, rows(b0 * 32, 32)] + zr2[k].astype(F32)
        g, u = total[:, :W], total[:, W:]
        s = 1.0 / (1.0 + jnp.exp(-g))
        hg[k, x, b1, b0] = (g * s * u).astype(BF)
        ha_copy(k, 0).start()
        h_copy(k, 7).wait_recv()
        grad = h32[k, x, b1, b0] + hz2[k].astype(F32)
        ag[k, x, b1, b0, :, :W] = (grad * u * s * (1.0 + g * (1.0 - s))).astype(BF)
        ag[k, x, b1, b0, :, W:] = (grad * g * s).astype(BF)
        for dz in (2, 1, 3):
            za_copy(k, dz).start()

    def s5(k):
        ha_copy(k, 0).wait_recv()
        ha_copy(k, 1).start()
        ha_copy(k, 2).start()
        for dz in (1, 2, 3):
            za_copy(k, dz).wait_recv()
        xa_copy(k, 0).start()
        xa_copy(k, 1).start()

    def s6(k):
        ha_copy(k, 1).wait_recv()
        ha_copy(k, 3).start()
        ha_copy(k, 2).wait_recv()
        ha_copy(k, 4).start()
        xa_copy(k, 0).wait_recv()
        xa_copy(k, 2).start()
        xa_copy(k, 1).wait_recv()
        xa_copy(k, 3).start()

    def s7(k):
        ha_copy(k, 3).wait_recv()
        ha_copy(k, 4).wait_recv()
        ha_copy(k, 5).start()
        add_token_grad(k)

    def deltas(k):
        return ag[k].reshape(512, 2 * W)

    def hidden(k):
        return hg[k].reshape(512, W)

    def add_token_grad(k):
        xa_copy(k, 2).wait_recv()
        xa_copy(k, 3).wait_recv()
        acc[1] += dot(deltas(k), wgu[k], NT)

    def add_layer_out(k):
        ha_copy(k, 5).wait_recv()
        acc[0] += dot(hidden(k), wd[k], NN)

    def weight_grads(k):
        go[k] = dot(tc[0].reshape(512, 512), deltas(k), TN).astype(BF)
        for i in range(2):
            out_remote(k, i).start()
            out_local(k, i).start()
        do[k] = dot(hidden(k), tc[1].reshape(512, 512), TN).astype(BF)
        out_remote(k, 2).start()
        out_local(k, 2).start()

    def s8(k):
        add_layer_out(k)
        weight_grads(k)

    def forward(h):
        for dy in (1, 3, 2):
            b_y(h, dy).wait_recv()
            b_co(((y + 4 - dy) % 4) * 2 + (zh if h == 0 else 1 - zh)).start()

    def early(k):
        weights_here(k)
        half(k, zh)

    b_zh().wait_recv()
    for dy in (1, 2, 3):
        b_y(1, dy).start()
    forward(0)
    b_co(y * 2 + 1 - zh).start()

    @pl.loop(AHEAD, EARLY + 1)
    def _(k):
        for d in w_remote(k):
            d.start()

    acc[...] = jnp.zeros_like(acc)
    for p in range(4):
        b_co(p * 2 + zh).wait_recv()
    pl.loop(0, EARLY // 2)(early)
    forward(1)
    pl.loop(EARLY // 2, EARLY)(early)
    for p in range(4):
        b_co(p * 2 + 1 - zh).wait_recv()

    @pl.loop(0, NP + 8)
    def _(t):
        @pl.when(t < NP - EARLY - 1)
        def _():
            for d in w_remote(t + EARLY + 1):
                d.start()

        for lag, stage in ((0, s0), (2, s1), (3, s2), (4, s3), (5, s4), (6, s5), (7, s6), (8, s7), (9, s8)):
            k = t - lag

            @pl.when((k >= 0) & (k < NP - (stage is s8)))
            def _(k=k, stage=stage):
                stage(k)

    def part(dy):
        return rows(((y + dy) % 4) * 128, 128)

    def e1(i, dy):
        src, dst = acc.at[i, part(dy), feats(1 - c)], e1b.at[i, part(dy)]
        return remote(src, dst, e1_s.at[i, dy], e1_r.at[i, dy], at_co)

    def e2(i, dy):
        src, n = e2b.at[i, part(dy)], dy - 1
        return remote(src, e2r.at[n, i], e2_s.at[i, n], e2_r.at[i, n], at_y(dy))

    def e3(i):
        return remote(e3b.at[i], e3r.at[i], e3_s.at[i], e3_r.at[i], at_zh)

    def over_cores(i):
        for dy in (2, 1, 3):
            e1(i, dy).wait_recv()
            e2b[i, part(dy)] = (acc[i, part(dy), feats(c)] + e1b[i, part(dy)]).astype(BF)
            e2(i, dy).start()

    for dy in (2, 1, 3, 0):
        e1(1, dy).start()
    over_cores(1)
    add_layer_out(NP - 1)
    for dy in (2, 1, 3, 0):
        e1(0, dy).start()
    over_cores(0)
    weight_grads(NP - 1)
    for i in (1, 0):
        e1(i, 0).wait_recv()
        e1b[i, part(0)] = acc[i, part(0), feats(c)] + e1b[i, part(0)]
    there, mine = rows(y * 128 + (1 - zh) * 64, 64), rows(y * 128 + zh * 64, 64)
    rt, rm = rows((1 - zh) * 64, 64), rows(zh * 64, 64)
    for i in (1, 0):
        for dy in (1, 3, 2):
            e2(i, dy).wait_recv()
        away = e1b[i, there]
        for n in range(3):
            away = away + e2r[n, i, rt].astype(F32)
        e3b[i] = away.astype(BF)
        e3(i).start()

    b_zh().wait_send()
    for h in (0, 1):
        for dy in (1, 2, 3):
            b_y(h, dy).wait_send()

    @pl.loop(0, 8)
    def _(j):
        b_co(j).wait_send()

    @pl.loop(0, NP)
    def _(k):
        for d in w_remote(k):
            d.wait_send()
        for i in range(6):
            x_copy(k, i).wait_send()
        for i in range(2):
            z_copy(k, i).wait_send()
        for dz in (1, 2, 3):
            za_copy(k, dz).wait_send()
        for i in range(4):
            xa_copy(k, i).wait_send()
        for i in range(9):
            h_copy(k, i).wait_send()
        for i in range(6):
            ha_copy(k, i).wait_send()
        for i in range(3):
            out_local(k, i).wait()
            out_remote(k, i).wait()

    for i, out in ((1, tg_ref), (0, lo_ref)):
        kept = e1b[i, mine]
        for n in range(3):
            kept = kept + e2r[n, i, rm].astype(F32)
        e3(i).wait_recv()
        out[...] = (kept + e3r[i].astype(F32)).astype(BF)

    for i in (0, 1):
        for dy in (0, 1, 2, 3):
            e1(i, dy).wait_send()
        for dy in (1, 2, 3):
            e2(i, dy).wait_send()
        e3(i).wait_send()


def finish(*refs):
    srcs, dsts, stage, ins, outs = refs[:5], refs[5:10], refs[10:15], refs[15], refs[16]
    pairs = []
    for a, b, m in zip(srcs, dsts, stage):
        n = 4 if a.shape[0] > 64 else 1
        step = a.shape[0] // n
        for i in range(n):
            part, k = pl.ds(i * step, step), len(pairs)
            pairs.append(
                (
                    pltpu.make_async_copy(a.at[part], m.at[part], ins.at[k]),
                    pltpu.make_async_copy(m.at[part], b.at[part], outs.at[k]),
                )
            )
    for first, _ in pairs:
        first.start()
    for first, second in pairs:
        first.wait()
        second.start()
    for _, second in pairs:
        second.wait()


def local(tokens, gate_weight, up_weight, down_weight, out_grad):
    def v(*shape, t=BF):
        return pltpu.VMEM(shape, t)

    def sem(*shape):
        return pltpu.SemaphoreType.DMA(shape) if shape else pltpu.SemaphoreType.DMA

    anywhere = pl.BlockSpec(memory_space=pl.ANY)
    vmem = pl.BlockSpec(memory_space=pltpu.VMEM)
    macs = 9 * 512 * 256 * 3584
    shapes = (
        jax.ShapeDtypeStruct((64, 256), BF),
        jax.ShapeDtypeStruct((64, 256), BF),
        jax.ShapeDtypeStruct((256, 3584), BF),
        jax.ShapeDtypeStruct((256, 3584), BF),
        jax.ShapeDtypeStruct((3584, 256), BF),
    )
    results = pl.pallas_call(
        kernel,
        out_shape=shapes,
        in_specs=[anywhere] * 5,
        out_specs=(vmem, vmem, anywhere, anywhere, anywhere),
        scratch_shapes=[
            v(2, 4, 2, 64, 512),
            v(NP, 512, 2 * W),
            v(NP, W, 512),
            v(NP, 4, 2, 64, 2 * W, t=F32),
            v(NP, 4, 2, 64, 2 * W),
            v(NP, 2, 64, 2 * W),
            v(NP, 2, 64, 2 * W),
            v(NP, 2, 2, 64, 2 * W),
            v(NP, 2, 2, 32, 2 * W),
            v(NP, 2, 32, 2 * W),
            v(NP, 32, 2 * W),
            v(NP, 32, 2 * W),
            v(NP, 4, 2, 2, 32, W, t=F32),
            v(NP, 4, 2, 2, 32, W),
            v(NP, 4, 2, 32, W),
            v(NP, 4, 2, 32, W),
            v(NP, 2, 32, W),
            v(NP, 2, 32, W),
            v(NP, 2, 2, 32, W),
            v(NP, 32, W),
            v(NP, 32, W),
            v(NP, 4, 2, 2, 32, 2 * W),
            v(NP, 4, 2, 2, 32, W),
            v(NP, 512, 2 * W),
            v(NP, W, 512),
            v(2, 512, 512, t=F32),
            v(2, 512, 256, t=F32),
            v(2, 512, 256),
            v(3, 2, 128, 256),
            v(2, 64, 256),
            v(2, 64, 256),
            sem(2), sem(NP, 3), sem(NP, 3), sem(NP, 3),
            sem(), sem(), sem(2, 3), sem(2, 3), sem(8), sem(8),
            sem(NP, 6), sem(NP, 6), sem(NP, 2), sem(NP, 2),
            sem(NP, 3), sem(NP, 3), sem(NP, 4), sem(NP, 4),
            sem(NP, 9), sem(NP, 9), sem(NP, 6), sem(NP, 6),
            sem(NP, 3), sem(NP, 3), sem(NP, 3),
            sem(2, 4), sem(2, 4), sem(2, 3), sem(2, 3), sem(2), sem(2),
        ],
        compiler_params=pltpu.CompilerParams(
            collective_id=0, has_side_effects=True, vmem_limit_bytes=60 * 2**20
        ),
        cost_estimate=pl.CostEstimate(flops=2 * macs, bytes_accessed=12 * 2**20, transcendentals=2**16),
        name="swiglu",
    )(tokens, gate_weight, up_weight, down_weight, out_grad)
    return pl.pallas_call(
        finish,
        out_shape=shapes,
        in_specs=[anywhere] * 5,
        out_specs=(anywhere,) * 5,
        scratch_shapes=[v(*a.shape) for a in shapes] + [sem(14), sem(14)],
        compiler_params=pltpu.CompilerParams(vmem_limit_bytes=60 * 2**20),
        cost_estimate=pl.CostEstimate(flops=0, bytes_accessed=12 * 2**20, transcendentals=0),
        name="finish",
    )(*results)


def solution(mesh):
    tokens, weights = P("col", "row"), P("row", "col")
    return jax.shard_map(
        local,
        mesh=mesh,
        in_specs=(tokens, weights, weights, tokens, tokens),
        out_specs=(tokens, tokens, weights, weights, tokens),
        check_vma=False,
    )
```

```python
import jax
import jax.numpy as jnp
from jax import lax
from jax.experimental import pallas as pl
from jax.experimental.pallas import tpu as pltpu
from jax.sharding import PartitionSpec as P

MESH = pl.DeviceIdType.MESH
BF = jnp.bfloat16
F32 = jnp.float32
NP = 7
W = 256
AHEAD = 1
EARLY = 4
HALF = NP * W
F = 256


def dot(a, b, dims):
    return lax.dot_general(a, b, (dims, ((), ())), preferred_element_type=F32)


NN = ((1,), (0,))
NT = ((1,), (1,))
TN = ((0,), (0,))


def kernel(
    tok, gate_w, up_w, down_w, cot,
    lo_ref, tg_ref, gate_g, up_g, down_g,
    tc, wgu, wd, s32, sb, r1, a2, r2, yb, zr1, yc, zr2,
    h32, hs, hz1, hb, hr1, ha, hr2, hy, hz2, ag, hg, go, do, acc, e1b, e2b, e2r, e3b, e3r,
    in_l, wl, ws, wr, zh_s, zh_r, y_s, y_r, co_s, co_r,
    x_s, x_r, z_s, z_r, za_s, za_r, xa_s, xa_r, h_s, h_r, ha_s, ha_r, ol, os_, or_,
    e1_s, e1_r, e2_s, e2_r, e3_s, e3_r,
):
    row, col = lax.axis_index("row"), lax.axis_index("col")
    x, zl, c = row // 8, (row // 2) % 4, row % 2
    y, zh = col // 2, col % 2
    xp, xm, x2 = (x + 1) % 4, (x + 3) % 4, (x + 2) % 4

    def at_x(px):
        return (px * 8 + zl * 2 + c, col)

    def z_of(dz):
        b = (zl % 2) if dz % 2 == 0 else 1 - zl % 2
        h = (zl // 2) if dz < 2 else 1 - zl // 2
        return h * 2 + b

    def at_z(dz):
        return (x * 8 + z_of(dz) * 2 + c, col)

    def at_y(dy):
        return (row, ((y + dy) % 4) * 2 + zh)

    at_co = (x * 8 + zl * 2 + 1 - c, col)
    at_zh = (row, y * 2 + 1 - zh)
    peers = [at_co, at_zh, at_x(xp), at_x(xm)]
    peers += [at_z(d) for d in (1, 2, 3)] + [at_y(d) for d in (1, 2, 3)]

    def remote(src, dst, ss, rs, dev):
        return pltpu.make_async_remote_copy(
            src_ref=src, dst_ref=dst, send_sem=ss, recv_sem=rs, device_id=dev, device_id_type=MESH
        )

    def cols(core, k):
        return pl.ds(pl.multiple_of(core * HALF + k * W, W), W)

    def feats(core):
        return pl.ds(pl.multiple_of(core * F, F), F)

    def rows(start, size):
        return pl.ds(pl.multiple_of(start, size), size)

    def w_local(k):
        return (
            pltpu.make_async_copy(gate_w.at[:, cols(c, k)], wgu.at[k, feats(c), pl.ds(0, W)], wl.at[k, 0]),
            pltpu.make_async_copy(up_w.at[:, cols(c, k)], wgu.at[k, feats(c), pl.ds(W, W)], wl.at[k, 1]),
            pltpu.make_async_copy(down_w.at[cols(c, k), :], wd.at[k, :, feats(c)], wl.at[k, 2]),
        )

    def w_remote(k):
        o = 1 - c
        return (
            remote(gate_w.at[:, cols(o, k)], wgu.at[k, feats(c), pl.ds(0, W)], ws.at[k, 0], wr.at[k, 0], at_co),
            remote(up_w.at[:, cols(o, k)], wgu.at[k, feats(c), pl.ds(W, W)], ws.at[k, 1], wr.at[k, 1], at_co),
            remote(down_w.at[cols(o, k), :], wd.at[k, :, feats(c)], ws.at[k, 2], wr.at[k, 2], at_co),
        )

    def block(j):
        return tc.at[:, j // 2, j % 2, :, feats(c)]

    def b_zh():
        return remote(block(col), block(col), zh_s, zh_r, at_zh)

    def b_y(h, dy):
        b = block(y * 2 + (zh if h == 0 else 1 - zh))
        return remote(b, b, y_s.at[h, dy - 1], y_r.at[h, dy - 1], at_y(dy))

    def b_co(j):
        return remote(block(j), block(j), co_s.at[j], co_r.at[j], at_co)

    ins = (
        pltpu.make_async_copy(tok, tc.at[0, y, zh, :, feats(c)], in_l.at[0]),
        pltpu.make_async_copy(cot, tc.at[1, y, zh, :, feats(c)], in_l.at[1]),
    )
    for d in ins:
        d.start()
    barrier = pltpu.get_barrier_semaphore()
    for p in peers:
        pl.semaphore_signal(barrier, inc=1, device_id=p, device_id_type=MESH)

    @pl.loop(0, NP)
    def _(k):
        for d in w_local(k):
            d.start()

    pl.semaphore_wait(barrier, len(peers))

    for d in ins:
        d.wait()
    b_zh().start()
    for dy in (1, 3, 2):
        b_y(0, dy).start()
    b_co(col).start()
    for k in range(AHEAD):
        for d in w_remote(k):
            d.start()

    b0, b1 = zl % 2, zl // 2

    def x_copy(k, i):
        if i == 0:
            src, dst, to = sb.at[k, x2, 0], r1.at[k, 0], xp
        elif i == 1:
            src, dst, to = sb.at[k, x2, 1], r1.at[k, 1], xm
        elif i == 2:
            src, dst, to = sb.at[k, xp, 1], r2.at[k, 0, 1], xp
        elif i == 3:
            src, dst, to = sb.at[k, xm, 0], r2.at[k, 1, 0], xm
        elif i == 4:
            src, dst, to = a2.at[k, 0], r2.at[k, 0, 0], xp
        else:
            src, dst, to = a2.at[k, 1], r2.at[k, 1, 1], xm
        return remote(src, dst, x_s.at[k, i], x_r.at[k, i], at_x(to))

    def z_copy(k, i):
        if i == 0:
            return remote(yb.at[k, :, 1 - b0], zr1.at[k], z_s.at[k, 0], z_r.at[k, 0], at_z(1))
        return remote(yc.at[k], zr2.at[k], z_s.at[k, 1], z_r.at[k, 1], at_z(2))

    def h_copy(k, i):
        to = xp if i in (1, 3, 5) else xm
        if i in (0, 8):
            src, dst = hs.at[k, :, i // 8, 1 - b0], hz1.at[k, :, i // 8]
        elif i == 1:
            src, dst = hb.at[k, x2, 0], hr1.at[k, 0]
        elif i == 2:
            src, dst = hb.at[k, x2, 1], hr1.at[k, 1]
        elif i == 3:
            src, dst = hb.at[k, xp, 1], hr2.at[k, 0, 1]
        elif i == 4:
            src, dst = hb.at[k, xm, 0], hr2.at[k, 1, 0]
        elif i == 5:
            src, dst = ha.at[k, 0], hr2.at[k, 0, 0]
        elif i == 6:
            src, dst = ha.at[k, 1], hr2.at[k, 1, 1]
        else:
            src, dst = hy.at[k], hz2.at[k]
        dev = at_z(1) if i in (0, 8) else at_z(2) if i == 7 else at_x(to)
        return remote(src, dst, h_s.at[k, i], h_r.at[k, i], dev)

    def za_copy(k, dz):
        part = ag.at[k, x, b1, b0]
        return remote(part, part, za_s.at[k, dz - 1], za_r.at[k, dz - 1], at_z(dz))

    def xa_copy(k, i):
        part = ag.at[k, x] if i < 2 else ag.at[k, xm, 0] if i == 2 else ag.at[k, xp, 1]
        return remote(part, part, xa_s.at[k, i], xa_r.at[k, i], at_x(xm if i % 2 else xp))

    def ha_copy(k, i):
        if i == 0:
            part, dev = hg.at[k, x, b1, b0], at_z(2)
        elif i == 1:
            part, dev = hg.at[k, x, :, b0], at_x(xp)
        elif i == 2:
            part, dev = hg.at[k, x, :, b0], at_x(xm)
        elif i == 3:
            part, dev = hg.at[k, xm, 0, b0], at_x(xp)
        elif i == 4:
            part, dev = hg.at[k, xp, 1, b0], at_x(xm)
        else:
            part, dev = hg.at[k, :, :, b0], at_z(1)
        return remote(part, part, ha_s.at[k, i], ha_r.at[k, i], dev)

    def out_refs(k, i, core):
        if i == 2:
            return do.at[k, :, feats(core)], down_g.at[cols(c, k), :]
        return go.at[k, feats(core), pl.ds(i * W, W)], (gate_g, up_g)[i].at[:, cols(c, k)]

    def out_local(k, i):
        return pltpu.make_async_copy(*out_refs(k, i, c), ol.at[k, i])

    def out_remote(k, i):
        return remote(*out_refs(k, i, 1 - c), os_.at[k, i], or_.at[k, i], at_co)

    def weights_here(k):
        for d in w_local(k):
            d.wait()
        for d in w_remote(k):
            d.wait_recv()

    def half(k, b):
        p = dot(tc[0, :, b].reshape(256, 512), wgu[k], NN).reshape(4, 64, 2 * W)
        s32[k, :, b] = p
        sb[k, :, b] = p.astype(BF)
        q = dot(tc[1, :, b].reshape(256, 512), wd[k], NT).reshape(4, 2, 32, W)
        h32[k, :, b] = q
        hs[k, :, b] = q.astype(BF)
        for which, sends in ((0, (0, 3, 0)), (1, (1, 2, 8))):

            @pl.when(b == which)
            def _(sends=sends):
                x_copy(k, sends[0]).start()
                x_copy(k, sends[1]).start()
                h_copy(k, sends[2]).start()

    def s0(k):
        @pl.when(k >= EARLY)
        def _():
            weights_here(k)
            half(k, zh)

        half(k, 1 - zh)

    def s1(k):
        x_copy(k, 0).wait_recv()
        a2[k, 0] = (s32[k, xp, 0] + r1[k, 0].astype(F32)).astype(BF)
        x_copy(k, 4).start()
        x_copy(k, 1).wait_recv()
        a2[k, 1] = (s32[k, xm, 1] + r1[k, 1].astype(F32)).astype(BF)
        x_copy(k, 5).start()
        h_copy(k, 0).wait_recv()
        h_copy(k, 8).wait_recv()
        half = h32[k, :, :, b0] + hz1[k].astype(F32)
        h32[k, :, :, b0] = half
        hb[k] = half.astype(BF)
        for i in (1, 2, 3, 4):
            h_copy(k, i).start()

    def s2(k):
        for i in (2, 3, 4, 5):
            x_copy(k, i).wait_recv()
        total = s32[k, x] + (r2[k, 0].astype(F32) + r2[k, 1].astype(F32))
        s32[k, x] = total
        yb[k] = total.astype(BF).reshape(2, 2, 32, 2 * W)
        z_copy(k, 0).start()
        h_copy(k, 1).wait_recv()
        ha[k, 0] = (h32[k, xp, 0, b0] + hr1[k, 0].astype(F32)).astype(BF)
        h_copy(k, 5).start()
        h_copy(k, 2).wait_recv()
        ha[k, 1] = (h32[k, xm, 1, b0] + hr1[k, 1].astype(F32)).astype(BF)
        h_copy(k, 6).start()

    def s3(k):
        z_copy(k, 0).wait_recv()
        mine = rows(b0 * 32, 32)
        yc[k] = (s32[k, x, 1 - b1, mine] + zr1[k, 1 - b1].astype(F32)).astype(BF)
        z_copy(k, 1).start()
        s32[k, x, b1, mine] = s32[k, x, b1, mine] + zr1[k, b1].astype(F32)
        for i in (3, 4, 5, 6):
            h_copy(k, i).wait_recv()
        total = h32[k, x, :, b0] + (hr2[k, 0].astype(F32) + hr2[k, 1].astype(F32))
        h32[k, x, :, b0] = total
        hy[k] = h32[k, x, 1 - b1, b0].astype(BF)
        h_copy(k, 7).start()

    def s4(k):
        z_copy(k, 1).wait_recv()
        total = s32[k, x, b1, rows(b0 * 32, 32)] + zr2[k].astype(F32)
        g, u = total[:, :W], total[:, W:]
        s = 1.0 / (1.0 + jnp.exp(-g))
        hg[k, x, b1, b0] = (g * s * u).astype(BF)
        ha_copy(k, 0).start()
        h_copy(k, 7).wait_recv()
        grad = h32[k, x, b1, b0] + hz2[k].astype(F32)
        ag[k, x, b1, b0, :, :W] = (grad * u * s * (1.0 + g * (1.0 - s))).astype(BF)
        ag[k, x, b1, b0, :, W:] = (grad * g * s).astype(BF)
        for dz in (2, 1, 3):
            za_copy(k, dz).start()

    def s5(k):
        ha_copy(k, 0).wait_recv()
        ha_copy(k, 1).start()
        ha_copy(k, 2).start()
        for dz in (1, 2, 3):
            za_copy(k, dz).wait_recv()
        xa_copy(k, 0).start()
        xa_copy(k, 1).start()

    def s6(k):
        ha_copy(k, 1).wait_recv()
        ha_copy(k, 3).start()
        ha_copy(k, 2).wait_recv()
        ha_copy(k, 4).start()
        xa_copy(k, 0).wait_recv()
        xa_copy(k, 2).start()
        xa_copy(k, 1).wait_recv()
        xa_copy(k, 3).start()

    def s7(k):
        ha_copy(k, 3).wait_recv()
        ha_copy(k, 4).wait_recv()
        ha_copy(k, 5).start()
        add_token_grad(k)

    def deltas(k):
        return ag[k].reshape(512, 2 * W)

    def hidden(k):
        return hg[k].reshape(512, W)

    def add_token_grad(k):
        xa_copy(k, 2).wait_recv()
        xa_copy(k, 3).wait_recv()
        acc[1] += dot(deltas(k), wgu[k], NT)

    def add_layer_out(k):
        ha_copy(k, 5).wait_recv()
        acc[0] += dot(hidden(k), wd[k], NN)

    def weight_grads(k):
        go[k] = dot(tc[0].reshape(512, 512), deltas(k), TN).astype(BF)
        for i in range(2):
            out_remote(k, i).start()
            out_local(k, i).start()
        do[k] = dot(hidden(k), tc[1].reshape(512, 512), TN).astype(BF)
        out_remote(k, 2).start()
        out_local(k, 2).start()

    def s8(k):
        add_layer_out(k)
        weight_grads(k)

    def forward(h):
        for dy in (1, 3, 2):
            b_y(h, dy).wait_recv()
            b_co(((y + 4 - dy) % 4) * 2 + (zh if h == 0 else 1 - zh)).start()

    def early(k):
        weights_here(k)
        half(k, zh)

    b_zh().wait_recv()
    for dy in (1, 2, 3):
        b_y(1, dy).start()
    forward(0)
    b_co(y * 2 + 1 - zh).start()

    @pl.loop(AHEAD, EARLY + 1)
    def _(k):
        for d in w_remote(k):
            d.start()

    acc[...] = jnp.zeros_like(acc)
    for p in range(4):
        b_co(p * 2 + zh).wait_recv()
    pl.loop(0, EARLY // 2)(early)
    forward(1)
    pl.loop(EARLY // 2, EARLY)(early)
    for p in range(4):
        b_co(p * 2 + 1 - zh).wait_recv()

    @pl.loop(0, NP + 8)
    def _(t):
        @pl.when(t < NP - EARLY - 1)
        def _():
            for d in w_remote(t + EARLY + 1):
                d.start()

        for lag, stage in ((0, s0), (2, s1), (3, s2), (4, s3), (5, s4), (6, s5), (7, s6), (8, s7), (9, s8)):
            k = t - lag

            @pl.when((k >= 0) & (k < NP - (stage is s8)))
            def _(k=k, stage=stage):
                stage(k)

    def part(dy):
        return rows(((y + dy) % 4) * 128, 128)

    def e1(i, dy):
        src, dst = acc.at[i, part(dy), feats(1 - c)], e1b.at[i, part(dy)]
        return remote(src, dst, e1_s.at[i, dy], e1_r.at[i, dy], at_co)

    def e2(i, dy):
        src, n = e2b.at[i, part(dy)], dy - 1
        return remote(src, e2r.at[n, i], e2_s.at[i, n], e2_r.at[i, n], at_y(dy))

    def e3(i):
        return remote(e3b.at[i], e3r.at[i], e3_s.at[i], e3_r.at[i], at_zh)

    def over_cores(i):
        for dy in (2, 1, 3):
            e1(i, dy).wait_recv()
            e2b[i, part(dy)] = (acc[i, part(dy), feats(c)] + e1b[i, part(dy)]).astype(BF)
            e2(i, dy).start()

    for dy in (2, 1, 3, 0):
        e1(1, dy).start()
    over_cores(1)
    add_layer_out(NP - 1)
    for dy in (2, 1, 3, 0):
        e1(0, dy).start()
    over_cores(0)
    weight_grads(NP - 1)
    for i in (1, 0):
        e1(i, 0).wait_recv()
        e1b[i, part(0)] = acc[i, part(0), feats(c)] + e1b[i, part(0)]
    there, mine = rows(y * 128 + (1 - zh) * 64, 64), rows(y * 128 + zh * 64, 64)
    rt, rm = rows((1 - zh) * 64, 64), rows(zh * 64, 64)
    for i in (1, 0):
        for dy in (1, 3, 2):
            e2(i, dy).wait_recv()
        away = e1b[i, there]
        for n in range(3):
            away = away + e2r[n, i, rt].astype(F32)
        e3b[i] = away.astype(BF)
        e3(i).start()

    b_zh().wait_send()
    for h in (0, 1):
        for dy in (1, 2, 3):
            b_y(h, dy).wait_send()

    @pl.loop(0, 8)
    def _(j):
        b_co(j).wait_send()

    @pl.loop(0, NP)
    def _(k):
        for d in w_remote(k):
            d.wait_send()
        for i in range(6):
            x_copy(k, i).wait_send()
        for i in range(2):
            z_copy(k, i).wait_send()
        for dz in (1, 2, 3):
            za_copy(k, dz).wait_send()
        for i in range(4):
            xa_copy(k, i).wait_send()
        for i in range(9):
            h_copy(k, i).wait_send()
        for i in range(6):
            ha_copy(k, i).wait_send()
        for i in range(3):
            out_local(k, i).wait()
            out_remote(k, i).wait()

    for i, out in ((1, tg_ref), (0, lo_ref)):
        kept = e1b[i, mine]
        for n in range(3):
            kept = kept + e2r[n, i, rm].astype(F32)
        e3(i).wait_recv()
        out[...] = (kept + e3r[i].astype(F32)).astype(BF)

    for i in (0, 1):
        for dy in (0, 1, 2, 3):
            e1(i, dy).wait_send()
        for dy in (1, 2, 3):
            e2(i, dy).wait_send()
        e3(i).wait_send()


def finish(*refs):
    srcs, dsts, stage, ins, outs = refs[:5], refs[5:10], refs[10:15], refs[15], refs[16]
    pairs = []
    for a, b, m in zip(srcs, dsts, stage):
        n = 4 if a.shape[0] > 64 else 1
        step = a.shape[0] // n
        for i in range(n):
            part, k = pl.ds(i * step, step), len(pairs)
            pairs.append(
                (
                    pltpu.make_async_copy(a.at[part], m.at[part], ins.at[k]),
                    pltpu.make_async_copy(m.at[part], b.at[part], outs.at[k]),
                )
            )
    for first, _ in pairs:
        first.start()
    for first, second in pairs:
        first.wait()
        second.start()
    for _, second in pairs:
        second.wait()


def local(tokens, gate_weight, up_weight, down_weight, out_grad):
    def v(*shape, t=BF):
        return pltpu.VMEM(shape, t)

    def sem(*shape):
        return pltpu.SemaphoreType.DMA(shape) if shape else pltpu.SemaphoreType.DMA

    anywhere = pl.BlockSpec(memory_space=pl.ANY)
    vmem = pl.BlockSpec(memory_space=pltpu.VMEM)
    macs = 9 * 512 * 256 * 3584
    shapes = (
        jax.ShapeDtypeStruct((64, 256), BF),
        jax.ShapeDtypeStruct((64, 256), BF),
        jax.ShapeDtypeStruct((256, 3584), BF),
        jax.ShapeDtypeStruct((256, 3584), BF),
        jax.ShapeDtypeStruct((3584, 256), BF),
    )
    results = pl.pallas_call(
        kernel,
        out_shape=shapes,
        in_specs=[anywhere] * 5,
        out_specs=(vmem, vmem, anywhere, anywhere, anywhere),
        scratch_shapes=[
            v(2, 4, 2, 64, 512),
            v(NP, 512, 2 * W),
            v(NP, W, 512),
            v(NP, 4, 2, 64, 2 * W, t=F32),
            v(NP, 4, 2, 64, 2 * W),
            v(NP, 2, 64, 2 * W),
            v(NP, 2, 64, 2 * W),
            v(NP, 2, 2, 64, 2 * W),
            v(NP, 2, 2, 32, 2 * W),
            v(NP, 2, 32, 2 * W),
            v(NP, 32, 2 * W),
            v(NP, 32, 2 * W),
            v(NP, 4, 2, 2, 32, W, t=F32),
            v(NP, 4, 2, 2, 32, W),
            v(NP, 4, 2, 32, W),
            v(NP, 4, 2, 32, W),
            v(NP, 2, 32, W),
            v(NP, 2, 32, W),
            v(NP, 2, 2, 32, W),
            v(NP, 32, W),
            v(NP, 32, W),
            v(NP, 4, 2, 2, 32, 2 * W),
            v(NP, 4, 2, 2, 32, W),
            v(NP, 512, 2 * W),
            v(NP, W, 512),
            v(2, 512, 512, t=F32),
            v(2, 512, 256, t=F32),
            v(2, 512, 256),
            v(3, 2, 128, 256),
            v(2, 64, 256),
            v(2, 64, 256),
            sem(2), sem(NP, 3), sem(NP, 3), sem(NP, 3),
            sem(), sem(), sem(2, 3), sem(2, 3), sem(8), sem(8),
            sem(NP, 6), sem(NP, 6), sem(NP, 2), sem(NP, 2),
            sem(NP, 3), sem(NP, 3), sem(NP, 4), sem(NP, 4),
            sem(NP, 9), sem(NP, 9), sem(NP, 6), sem(NP, 6),
            sem(NP, 3), sem(NP, 3), sem(NP, 3),
            sem(2, 4), sem(2, 4), sem(2, 3), sem(2, 3), sem(2), sem(2),
        ],
        compiler_params=pltpu.CompilerParams(
            collective_id=0, has_side_effects=True, vmem_limit_bytes=60 * 2**20
        ),
        cost_estimate=pl.CostEstimate(flops=2 * macs, bytes_accessed=12 * 2**20, transcendentals=2**16),
        name="swiglu",
    )(tokens, gate_weight, up_weight, down_weight, out_grad)
    return pl.pallas_call(
        finish,
        out_shape=shapes,
        in_specs=[anywhere] * 5,
        out_specs=(anywhere,) * 5,
        scratch_shapes=[v(*a.shape) for a in shapes] + [sem(14), sem(14)],
        compiler_params=pltpu.CompilerParams(vmem_limit_bytes=60 * 2**20),
        cost_estimate=pl.CostEstimate(flops=0, bytes_accessed=12 * 2**20, transcendentals=0),
        name="finish",
    )(*results)


def solution(mesh):
    tokens, weights = P("col", "row"), P("row", "col")
    return jax.shard_map(
        local,
        mesh=mesh,
        in_specs=(tokens, weights, weights, tokens, tokens),
        out_specs=(tokens, tokens, weights, weights, tokens),
        check_vma=False,
    )
```
